32 devices in a mesh: shard: 4 (over y, core), ctx: 4 (over z), tp: 2 (over x).
Axes of the slice: x: 2, y: 2, z: 4, core: 2. Of those that a mesh axis runs over, the one named last changes fastest.
Arguments:
- stream: bfloat16 [8, 1024, 2048], P('shard', 'ctx', 'tp'), may hold values from -14 to 14
- norm_gain: float32 [2048], replicated, may hold values from 0.5 to 1.5
- in_weight: bfloat16 [2, 2048, 2, 4096], P(None, 'shard', None, 'tp'), may hold values from -0.125 to 0.125
- select_weight: bfloat16 [2, 160, 4096], P(None, 'shard', 'tp'), may hold values from -0.09375 to 0.09375
- delta_weight: bfloat16 [2, 128, 4096], P(None, 'shard', 'tp'), may hold values from -0.5 to 0.5
- delta_bias: float32 [2, 4096], P(None, 'tp'), may hold values from -6.9 to -2.3
- out_weight: bfloat16 [4096, 2048], P('tp', 'shard'), may hold values from -0.375 to 0.375
- filter_weight: float32 [4, 4096], P(None, 'tp'), may hold values from -3 to 3
- filter_bias: float32 [4096], P('tp'), may hold values from -0.5 to 0.5
- decay_log: float32 [16, 4096], P(None, 'tp'), may hold values from -1 to 2.5
- skip_gain: float32 [4096], P('tp'), may hold values from 0.5 to 1.5
- segments: int32 [8, 1024], P('shard'), may hold values from 0 to 3, never falling along the last dimension, each value on 1 to 800 neighbouring positions
- modality: int32 [8, 1024], P('shard', 'ctx'), may hold values from 0 to 1
- valid: int32 [8, 1024], P('shard', 'ctx'), may hold values 0 or 1
- upstream: bfloat16 [8, 1024, 2048], P('shard', 'ctx', 'tp'), may hold values from -6 to 6
Outputs:
- output: bfloat16 [8, 1024, 2048], P('shard', 'ctx', 'tp')
- stream_gradient: bfloat16 [8, 1024, 2048], P('shard', 'ctx', 'tp')
- gain_gradient: float32 [2048], P('tp')
- in_gradient: float32 [2, 2048, 2, 4096], P(None, ('shard', 'ctx'), None, 'tp')
- select_gradient: float32 [2, 160, 4096], P(None, ('shard', 'ctx'), 'tp')
- delta_gradient: float32 [2, 128, 4096], P(None, ('shard', 'ctx'), 'tp')
- bias_gradient: float32 [2, 4096], P(None, 'tp')
- out_gradient: float32 [4096, 2048], P('tp', ('shard', 'ctx'))
- filter_gradient: float32 [4, 4096], P(None, 'tp')
- offset_gradient: float32 [4096], P('tp')
- decay_gradient: float32 [16, 4096], P(None, 'tp')
- skip_gradient: float32 [4096], P('tp')
- stream_rms: float32 [], replicated
- mixer_rms: float32 [], replicated
The draws below stay inside these ranges and needn't reach their ends.
Inputs may be any that keep to these rules, and one draw needn't show every extreme that they name: `segments`: in each sequence segment numbers start at 0 and never fall; each document covers 1 to 800 positions.
All inputs are finite; a program needn't handle non-finite values. No bound on the sum of `valid` on one device may be relied on, other than what follows from the above.
Results may differ from the reference program's by a relative error of at most 0.012.
Values may be sent and summed in bfloat16 or wider, within the bound.
A program may use at most 384 MiB of HBM per device.

```python
import math
import jax
import jax.numpy as jnp
import numpy as np
from jax import lax

D = 2048
INNER = 4096
STATE = 16
RANK = 128
KERNEL = 4
MODES = 2
LEN = 1024
SEQS = 8
XW = 160


def draw_stream(key, part):
    seq_pos = jnp.arange(SEQS, dtype=jnp.float32)[:, None, None] / max(SEQS - 1, 1)
    tok_pos = jnp.arange(LEN, dtype=jnp.float32)[None, :, None] / max(LEN - 1, 1)
    col_pos = jnp.arange(D, dtype=jnp.float32)[None, None, :] / max(D - 1, 1)
    ramp = seq_pos + tok_pos + col_pos - 1.5
    base = jnp.clip(jax.random.normal(key, (SEQS, LEN, D), jnp.float32), -6.0, 6.0)
    scale = jnp.exp(0.5 * math.log(3.0) * ramp)
    return (base * scale).astype(jnp.bfloat16)


def touch_ends(entries, key, smallest, largest):
    longest = entries.shape.index(max(entries.shape))
    spots = []
    for shift in (0, 1):
        where = [jax.random.randint(jax.random.fold_in(key, axis), (), 0, length) for axis, length in enumerate(entries.shape)]
        where[longest] = (where[longest] + shift) % entries.shape[longest]
        spots.append(tuple(where))
    return entries.at[spots[0]].set(smallest).at[spots[1]].set(largest)


def level_of(rng, dims, cuts, smallest, high):
    def one(dim, parts):
        draws = jax.random.uniform(jax.random.fold_in(jax.random.fold_in(rng, 6), dim), (parts,), jnp.float32, smallest / len(cuts), high / len(cuts))
        return jnp.repeat(jnp.exp(draws), dims[dim] // parts).reshape((-1,) + (1,) * (len(dims) - dim - 1))

    level = one(*cuts[0])
    for cut in cuts[1:]:
        level = level * one(*cut)
    return level


def split_up(amount, total, bound, skew):
    weights = [(1 << 20) // math.isqrt(grade ** skew) + 1 for grade in range(2, amount + 1)]
    rest, counts = total - bound - (amount - 1), [1] * (amount - 1)
    while rest > 0:
        movable = [i for i in range(amount - 1) if counts[i] < bound]
        pool, remaining = sum([weights[i] for i in movable]), rest
        for i in movable:
            addition = min(bound - counts[i], max(1, remaining * weights[i] // pool), rest)
            counts[i] = counts[i] + addition
            rest = rest - addition
    return np.array([bound] + counts)


def uneven(rng, count, total, limit, slope):
    if count == 2:
        one = jax.random.randint(rng, (), max(1, total - limit), min(limit, total - 1) + 1)
        return jnp.stack([one, total - one])
    tallies = jnp.asarray(split_up(count, total, limit, slope), jnp.int32)
    twos = (count - 1) // 2
    giver, receiver = tallies[1:1 + 2 * twos:2], tallies[2:2 + 2 * twos:2]
    room = jnp.minimum(giver - 1, limit - receiver)
    shifted = jax.random.randint(jax.random.fold_in(rng, 1), (twos,), 0, 1 << 20) % (room + 1)
    tallies = tallies.at[1:1 + 2 * twos:2].set(giver - shifted).at[2:2 + 2 * twos:2].set(receiver + shifted)
    return tallies[jax.random.permutation(jax.random.fold_in(rng, 2), count)]


def normal_values(key, shape, scale, bound, cuts=(), kind=jnp.bfloat16):
    loudness = level_of(key, shape, cuts, -0.22, 0.18) if cuts else 1.0
    array = jax.random.normal(key, shape, jnp.float32) * scale * loudness
    return jnp.minimum(jnp.maximum(array, -bound), bound).astype(kind)


def setup_inputs(seed: int = 0) -> dict:
    splits = jax.random.split(jax.random.key(seed), 16)
    stream = draw_stream(jax.random.fold_in(splits[15], 71), 0)
    norm_gain = jnp.clip(1.0 + 0.1 * jax.random.normal(splits[1], (D,), jnp.float32), 0.5, 1.5)
    in_weight = normal_values(splits[2], (MODES, D, 2, INNER), D ** -0.5, 0.125, ((1, 4), (3, 2)))
    select_weight = normal_values(splits[3], (MODES, XW, INNER), INNER ** -0.5, 0.09375, ((1, 4), (2, 2)))
    delta_weight = normal_values(splits[4], (MODES, RANK, INNER), RANK ** -0.5, 0.5, ((1, 4), (2, 2)))
    delta_bias = jnp.clip(-6.9 + 4.6000001430511475 * jax.random.uniform(splits[5], (MODES, INNER), jnp.float32) ** level_of(splits[5], (MODES, INNER), ((1, 2),), -0.2, 0.2), -6.9, -2.3)
    out_weight = normal_values(splits[6], (INNER, D), (INNER // 16) ** -0.5, 0.375, ((0, 2), (1, 4)))
    filter_weight = normal_values(splits[7], (KERNEL, INNER), KERNEL ** -0.5, 3.0, ((1, 2),), jnp.float32)
    filter_bias = jnp.clip(jax.random.uniform(splits[8], (INNER,), jnp.float32, -0.5, 0.5) * level_of(splits[8], (INNER,), ((0, 2),), -0.4, 0.0), -0.5, 0.5)
    decay_log = jnp.clip(-1.0 + 3.5 * jax.random.uniform(splits[9], (STATE, INNER), jnp.float32) ** level_of(splits[9], (STATE, INNER), ((1, 2),), -0.2, 0.2), -1.0, 2.5)
    skip_gain = jnp.clip(0.5 + 1.0 * jax.random.uniform(splits[10], (INNER,), jnp.float32) ** level_of(splits[10], (INNER,), ((0, 2),), -0.2, 0.2), 0.5, 1.5)
    segments = jax.vmap(lambda own: jnp.searchsorted(jnp.cumsum(uneven(own, max(2, LEN // 256), LEN, LEN * 25 // 32, 0)), jnp.arange(LEN), side="right"))(jax.random.split(splits[11], SEQS)).reshape((SEQS, LEN)).astype(jnp.int32)
    modality = touch_ends(jax.random.randint(splits[12], (SEQS, LEN), 0, MODES), jax.random.fold_in(splits[12], 1), 0, MODES - 1).astype(jnp.int32)
    valid = touch_ends((jax.random.randint(splits[13], (SEQS, LEN), 0, 8) < 7).astype(jnp.int32), jax.random.fold_in(splits[13], 1), 0, 1)
    upstream = normal_values(splits[14], (SEQS, LEN, D), 1.0, 6.0, ((0, 4), (1, 4), (2, 2)))
    return {"stream": stream, "norm_gain": norm_gain, "in_weight": in_weight, "select_weight": select_weight, "delta_weight": delta_weight, "delta_bias": delta_bias, "out_weight": out_weight, "filter_weight": filter_weight, "filter_bias": filter_bias, "decay_log": decay_log, "skip_gain": skip_gain, "segments": segments, "modality": modality, "valid": valid, "upstream": upstream}


EPSILON = 1e-05

@jax.custom_vjp
def low(v):
    return lax.optimization_barrier(v.astype(jnp.bfloat16)).astype(jnp.float32)

@jax.custom_vjp
def low_back(v):
    return v

def low_keep(v):
    return (low(v), None)

def low_pass(kept, grad):
    return (grad,)

def back_keep(v):
    return (v, None)

def back_low(kept, grad):
    return (low(grad),)
low.defvjp(low_keep, low_pass)
low_back.defvjp(back_keep, back_low)

def highest(left, right):
    return jnp.dot(left, right, precision=lax.Precision.HIGHEST, preferred_element_type=jnp.float32)

def by_modality(values, weights, modes):
    total = highest(values, weights[0])
    for index in range(1, weights.shape[0]):
        total = jnp.where((modes == index)[:, None], highest(values, weights[index]), total)
    return total

def scan_block(carry, inputs, neg_decay):

    def advance(status, item):
        delta, signal, b_in, c_out, keep = item
        decay = jnp.exp(delta[:, None, :] * neg_decay[None]) * keep[:, None, None]
        status = decay * status + (delta * signal)[:, None, :] * b_in[:, :, None]
        return (status, lax.optimization_barrier(jnp.sum(status * c_out[:, :, None], axis=1)))
    return lax.scan(advance, carry, inputs, unroll=8)

def run_scan(delta, signal, b_in, c_out, keep, neg_decay, start):
    length = delta.shape[1]
    block = math.gcd(length, 64)

    def time_major(value):
        moved = jnp.moveaxis(value, 1, 0)
        return moved.reshape((length // block, block) + moved.shape[1:])
    blocks = tuple((time_major(value) for value in (delta, signal, b_in, c_out, keep)))
    blockwise = jax.checkpoint(scan_block)

    def outer(status, item):
        return blockwise(status, item, neg_decay)
    final, outputs = lax.scan(outer, start, blocks)
    outputs = outputs.reshape((length,) + outputs.shape[2:])
    return (jnp.moveaxis(outputs, 0, 1), final)

def layer(stream, norm_gain, in_weight, select_weight, delta_weight, delta_bias, out_weight, filter_weight, filter_bias, decay_log, skip_gain, segments, modality, valid):
    seqs, length, width = stream.shape
    inner = out_weight.shape[0]
    rank = delta_weight.shape[1]
    state = decay_log.shape[0]
    reach = filter_weight.shape[0] - 1
    modes = modality.reshape(-1)
    mean_sq = lax.optimization_barrier(jnp.mean(stream * stream, axis=2, keepdims=True))
    normed = low(stream * lax.rsqrt(mean_sq + EPSILON) * norm_gain)
    rows = normed.reshape(seqs * length, width)
    projected = low_back(by_modality(rows, in_weight.reshape(in_weight.shape[0], width, 2 * inner), modes))
    conv_in = low(projected[:, :inner]).reshape(seqs, length, inner)
    gate_in = projected[:, inner:]
    padded = jnp.pad(conv_in, ((0, 0), (reach, 0), (0, 0)))
    seg_pad = jnp.concatenate([jnp.full((seqs, reach), -1, jnp.int32), segments.astype(jnp.int32)], axis=1)
    pre = jnp.zeros((seqs, length, inner), jnp.float32) + filter_bias
    keep = None
    for lag in range(reach + 1):
        same = (seg_pad[:, reach - lag:reach - lag + length] == segments).astype(jnp.float32)
        if lag == 1:
            keep = same
        pre = pre + filter_weight[reach - lag] * padded[:, reach - lag:reach - lag + length] * same[:, :, None]
    conv_out = low(jax.nn.silu(pre)).reshape(seqs * length, inner)
    selected = low_back(by_modality(conv_out, jnp.swapaxes(select_weight, 1, 2), modes))
    delta_low = low(selected[:, :rank])
    b_in = selected[:, rank:rank + state]
    c_out = selected[:, rank + state:]
    bias_rows = delta_bias[0][None, :] + jnp.zeros((seqs * length, inner), jnp.float32)
    for index in range(1, delta_bias.shape[0]):
        bias_rows = jnp.where((modes == index)[:, None], delta_bias[index][None, :], bias_rows)
    delta = jax.nn.softplus(low_back(by_modality(delta_low, delta_weight, modes) + bias_rows))
    neg_decay = -jnp.exp(decay_log)
    start = jnp.zeros((seqs, state, inner), jnp.float32)
    scanned, final = run_scan(delta.reshape(seqs, length, inner), conv_out.reshape(seqs, length, inner), b_in.reshape(seqs, length, state), c_out.reshape(seqs, length, state), keep, neg_decay, start)
    mixed = scanned.reshape(seqs * length, inner) + skip_gain * conv_out
    gated = low(mixed * jax.nn.silu(gate_in))
    mix = low_back(highest(gated, out_weight)) * valid.reshape(-1)[:, None]
    return mix.reshape(seqs, length, width)

def reference(stream, norm_gain, in_weight, select_weight, delta_weight, delta_bias, out_weight, filter_weight, filter_bias, decay_log, skip_gain, segments, modality, valid, upstream):
    seqs, length, width = stream.shape
    group = math.gcd(seqs, max(1, 4096 // length))
    params = tuple((p.astype(jnp.float32) for p in (norm_gain, in_weight, select_weight, delta_weight, delta_bias, out_weight, filter_weight, filter_bias, decay_log, skip_gain)))
    valid_float = valid.astype(jnp.float32)

    def split(value):
        return value.reshape((seqs // group, group) + value.shape[1:])
    items = (split(stream.astype(jnp.float32)), split(segments), split(modality), split(valid_float), split(upstream.astype(jnp.float32)))

    def one(total, item):
        piece, seg, mode, flag, cotangent = item

        def forward(values, *weights):
            return layer(values, *weights, seg, mode, flag)
        mix, pull = jax.vjp(forward, piece, *params)
        grads = pull(cotangent)
        total = tuple((a + b for a, b in zip(total, grads[1:])))
        result = (piece + mix).astype(jnp.bfloat16)
        back = (cotangent + grads[0]).astype(jnp.bfloat16)
        stream_sq = jnp.sum(flag[:, :, None] * piece * piece)
        mixer_sq = jnp.sum(mix * mix)
        return (total, (result, back, stream_sq, mixer_sq))
    init = tuple((jnp.zeros_like(p) for p in params))
    total, (result, back, stream_sq, mixer_sq) = lax.scan(one, init, items)
    count = jnp.maximum(jnp.sum(valid_float), 1.0) * width
    stream_rms = jnp.sqrt(jnp.sum(stream_sq) / count)
    mixer_rms = jnp.sqrt(jnp.sum(mixer_sq) / count)
    output = result.reshape(seqs, length, width)
    stream_gradient = back.reshape(seqs, length, width)
    return (output, stream_gradient, total[0], total[1], total[2], total[3], total[4], total[5], total[6], total[7], total[8], total[9], stream_rms, mixer_rms)
```

```python
import functools
import jax
import jax.numpy as jnp
from jax import lax
from jax.experimental import pallas as pl
from jax.experimental.pallas import tpu as pltpu

LOG2E = 1.4426950408889634
VMEM_LIMIT = 60 * 1024 * 1024


def sigmoid(value):
    return 1.0 / (1.0 + jnp.exp(-value))


def softplus(value):
    return jnp.maximum(value, 0.0) + jnp.log1p(jnp.exp(-jnp.abs(value)))


def stage_rows(raw_ref, conv_ref, gate_ref, gg_ref, delta_s, conv_s, g_s, groups):
    def step(block, _):
        top = pl.multiple_of(block * 16, 16)
        for group in range(groups):
            lanes = slice(group * 128, group * 128 + 128)
            delta = softplus(raw_ref[pl.ds(top, 16), lanes])
            conv = conv_ref[pl.ds(top, 16), lanes].astype(jnp.float32)
            gate = gate_ref[pl.ds(top, 16), lanes]
            g_mixed = gg_ref[pl.ds(top, 16), lanes] * (gate * sigmoid(gate))
            for part in range(2):
                rows = pl.ds(pl.multiple_of(((block * 2 + part) * groups + group) * 8, 8), 8)
                eight = slice(part * 8, part * 8 + 8)
                delta_s[rows, :] = delta[eight]
                conv_s[rows, :] = conv[eight]
                g_s[rows, :] = g_mixed[eight]
        return 0

    lax.fori_loop(0, raw_ref.shape[0] // 16, step, 0)


def ends_kernel(groups, states, split, raw_ref, conv_ref, gate_ref, gg_ref, a_ref, b_ref, c_ref,
                cut_ref, h_ref, p_ref, l_ref, delta_s, conv_s, g_s):
    tokens = raw_ref.shape[0]
    first = pl.program_id(0) * tokens
    stage_rows(raw_ref, conv_ref, gate_ref, gg_ref, delta_s, conv_s, g_s, groups)
    for low in range(0, states, split):
        names = range(low, low + split)

        def eight_tokens(tile, carry):
            h, p, l = (list(part) for part in carry)
            for i in range(8):
                rows = pl.ds(tile * (groups * 8) + i, groups, stride=8)
                delta = delta_s[rows, :]
                signal = delta * conv_s[rows, :]
                g = g_s[rows, :]
                token = first + tile * 8 + i
                reach = delta + cut_ref[token]
                for k, n in enumerate(names):
                    decay = jnp.exp2(reach * a_ref[n])
                    h[k] = decay * h[k] + signal * b_ref[token * states + n]
                    p[k] = decay * p[k]
                    l[k] = l[k] + p[k] * (g * c_ref[token * states + n])
            return tuple(h), tuple(p), tuple(l)

        zero = tuple(jnp.zeros((groups, 128), jnp.float32) for _ in names)
        one = tuple(jnp.ones((groups, 128), jnp.float32) for _ in names)
        h, p, l = lax.fori_loop(0, tokens // 8, eight_tokens, (zero, one, zero))
        for k, n in enumerate(names):
            h_ref[n], p_ref[n], l_ref[n] = h[k], p[k], l[k]


def scan_kernel(groups, states, fsplit, bsplit, raw_ref, conv_ref, gate_ref, gg_ref, skip_ref, a_ref, h0_ref,
                q0_ref, b_ref, c_ref, cut_ref, gated_ref, ggate_ref, graw_ref, gconv_ref,
                ga_ref, gb_ref, gc_ref, gskip_ref, delta_s, conv_s, g_s, y_s, gs_s, h_s):
    tokens = raw_ref.shape[0]
    tiles = tokens // 8
    first = pl.program_id(0) * tokens
    stage_rows(raw_ref, conv_ref, gate_ref, gg_ref, delta_s, conv_s, g_s, groups)
    lane = lax.broadcasted_iota(jnp.int32, (groups, 128), 1)

    def split_sum(total, names, values, i):
        for n, value in zip(names, values):
            total = jnp.where(lane == i * states + n, jnp.sum(value, axis=1, keepdims=True), total)
        return total

    for low in range(0, states, fsplit):
        names = range(low, low + fsplit)

        def forward(tile, h):
            h = list(h)
            gc = jnp.zeros((groups, 128), jnp.float32) if low == 0 else gc_ref[tile]
            for i in range(8):
                rows = pl.ds(tile * (groups * 8) + i, groups, stride=8)
                delta = delta_s[rows, :]
                signal = delta * conv_s[rows, :]
                g = g_s[rows, :]
                token = tile * 8 + i
                at = (first + token) * states
                reach = delta + cut_ref[first + token]
                y = None
                parts = []
                for k, n in enumerate(names):
                    h_s[token, n] = h[k]
                    decay = jnp.exp2(reach * a_ref[n])
                    h[k] = decay * h[k] + signal * b_ref[at + n]
                    term = h[k] * c_ref[at + n]
                    y = term if y is None else y + term
                    parts.append(h[k] * g)
                gc = split_sum(gc, names, parts, i)
                y_s[rows, :] = y if low == 0 else y + y_s[rows, :]
            gc_ref[tile] = gc
            return tuple(h)

        lax.fori_loop(0, tiles, forward, tuple(h0_ref[n] for n in names))

    def between(block, total):
        top = pl.multiple_of(block * 16, 16)
        new = []
        for group in range(groups):
            lanes = slice(group * 128, group * 128 + 128)
            gate = gate_ref[pl.ds(top, 16), lanes]
            sig = sigmoid(gate)
            y, conv, g = (
                jnp.concatenate([ref[pl.ds(pl.multiple_of(((block * 2 + part) * groups + group) * 8, 8), 8), :]
                                 for part in range(2)], axis=0)
                for ref in (y_s, conv_s, g_s)
            )
            mixed = y + skip_ref[:, lanes] * conv
            gated_ref[pl.ds(top, 16), lanes] = (mixed * (gate * sig)).astype(jnp.bfloat16)
            g_gate = gg_ref[pl.ds(top, 16), lanes] * mixed * sig * (1.0 + gate * (1.0 - sig))
            ggate_ref[pl.ds(top, 16), lanes] = g_gate.astype(jnp.bfloat16)
            product = g * conv
            new.append(total[group] + product[:8] + product[8:])
        return tuple(new)

    sums = lax.fori_loop(0, tokens // 16, between,
                         tuple(jnp.zeros((8, 128), jnp.float32) for _ in range(groups)))
    for group in range(groups):
        gskip_ref[:, group * 128:group * 128 + 128] = sums[group]

    for low in range(0, states, bsplit):
        names = range(low, low + bsplit)

        def backward(step, carry):
            q, ga = (list(part) for part in carry)
            tile = tiles - 1 - step
            gb = jnp.zeros((groups, 128), jnp.float32) if low == 0 else gb_ref[tile]
            for i in reversed(range(8)):
                rows = pl.ds(tile * (groups * 8) + i, groups, stride=8)
                delta = delta_s[rows, :]
                conv = conv_s[rows, :]
                signal = delta * conv
                g = g_s[rows, :]
                token = tile * 8 + i
                at = (first + token) * states
                reach = delta + cut_ref[first + token]
                gd = gs = None
                parts = []
                for k, n in enumerate(names):
                    decay = jnp.exp2(reach * a_ref[n])
                    lam = q[k] + g * c_ref[at + n]
                    q[k] = decay * lam
                    w = q[k] * h_s[token, n]
                    ga[k] = ga[k] + w * delta
                    d_term = w * a_ref[n]
                    s_term = lam * b_ref[at + n]
                    gd = d_term if gd is None else gd + d_term
                    gs = s_term if gs is None else gs + s_term
                    parts.append(lam * signal)
                gb = split_sum(gb, names, parts, i)
                y_s[rows, :] = gd if low == 0 else gd + y_s[rows, :]
                gs_s[rows, :] = gs if low == 0 else gs + gs_s[rows, :]
            gb_ref[tile] = gb
            return tuple(q), tuple(ga)

        zero = tuple(jnp.zeros((groups, 128), jnp.float32) for _ in names)
        _, ga = lax.fori_loop(0, tiles, backward, (tuple(q0_ref[n] for n in names), zero))
        for k, n in enumerate(names):
            ga_ref[n] = ga[k]

    def after(block, _):
        top = pl.multiple_of(block * 16, 16)
        for group in range(groups):
            lanes = slice(group * 128, group * 128 + 128)
            raw = raw_ref[pl.ds(top, 16), lanes]
            gd, gs, conv, delta, g = (
                jnp.concatenate([ref[pl.ds(pl.multiple_of(((block * 2 + part) * groups + group) * 8, 8), 8), :]
                                 for part in range(2)], axis=0)
                for ref in (y_s, gs_s, conv_s, delta_s, g_s)
            )
            g_delta = gd * (1.0 / LOG2E) + conv * gs
            graw_ref[pl.ds(top, 16), lanes] = (g_delta * sigmoid(raw)).astype(jnp.bfloat16)
            gconv_ref[pl.ds(top, 16), lanes] = skip_ref[:, lanes] * g + delta * gs
        return 0

    lax.fori_loop(0, tokens // 16, after, 0)


def sizes(raw, seqs, states):
    rows, inner = raw.shape
    groups = min(8, inner // 128)
    return rows // seqs, inner // (groups * 128), groups


def state_form(value, blocks, groups):
    states = value.shape[0]
    return value.reshape(states, blocks, groups, 128).transpose(1, 0, 2, 3)


def from_state_form(value):
    blocks, states, groups, lanes = value.shape
    return value.transpose(1, 0, 2, 3).reshape(states, blocks * groups * lanes)


def token_spec(tokens, width):
    return pl.BlockSpec((tokens, width), lambda s, j: (s, j))


def state_spec(states, groups):
    return pl.BlockSpec((None, None, states, groups, 128), lambda s, j: (s, j, 0, 0, 0))


def scan_ends(raw, conv, gate, gg, a2, b, c, cut, seqs, split=16):
    blocks, states, groups, _ = a2.shape
    tokens, _, _ = sizes(raw, seqs, states)
    width = groups * 128
    smem = pl.BlockSpec(memory_space=pltpu.SMEM)
    out = jax.ShapeDtypeStruct((seqs, blocks, states, groups, 128), jnp.float32)
    elements = raw.size * states
    return pl.pallas_call(
        functools.partial(ends_kernel, groups, states, min(split, states)),
        grid=(seqs, blocks),
        in_specs=[token_spec(tokens, width)] * 4
        + [pl.BlockSpec((None, states, groups, 128), lambda s, j: (j, 0, 0, 0)), smem, smem, smem],
        out_specs=[state_spec(states, groups)] * 3,
        out_shape=[out] * 3,
        scratch_shapes=[pltpu.VMEM((tokens * groups, 128), jnp.float32)] * 3,
        compiler_params=pltpu.CompilerParams(vmem_limit_bytes=VMEM_LIMIT),
        cost_estimate=pl.CostEstimate(flops=8 * elements, bytes_accessed=14 * raw.size, transcendentals=elements),
        name="scan_ends",
    )(raw, conv, gate, gg, a2, b.reshape(-1), c.reshape(-1), cut.reshape(-1))


def scan_both(raw, conv, gate, gg, skip, a2, h0, q0, b, c, cut, seqs, fsplit=16, bsplit=16):
    blocks, states, groups, _ = a2.shape
    rows, inner = raw.shape
    tokens, _, _ = sizes(raw, seqs, states)
    width = groups * 128
    smem = pl.BlockSpec(memory_space=pltpu.SMEM)
    elements = raw.size * states
    token = token_spec(tokens, width)
    tiles = tokens // 8
    pair = pl.BlockSpec((None, tiles, groups, 128), lambda s, j: (j, s, 0, 0))
    pair_shape = jax.ShapeDtypeStruct((blocks, rows // 8, groups, 128), jnp.float32)
    low = jax.ShapeDtypeStruct((rows, inner), jnp.bfloat16)
    return pl.pallas_call(
        functools.partial(scan_kernel, groups, states, min(fsplit, states), min(bsplit, states)),
        grid=(seqs, blocks),
        in_specs=[token] * 4
        + [pl.BlockSpec((1, width), lambda s, j: (0, j)),
           pl.BlockSpec((None, states, groups, 128), lambda s, j: (j, 0, 0, 0)),
           state_spec(states, groups), state_spec(states, groups), smem, smem, smem],
        out_specs=[token] * 4 + [state_spec(states, groups), pair, pair,
                                 pl.BlockSpec((None, 8, width), lambda s, j: (s, 0, j))],
        out_shape=[low, low, low, jax.ShapeDtypeStruct((rows, inner), jnp.float32),
                   jax.ShapeDtypeStruct((seqs, blocks, states, groups, 128), jnp.float32),
                   pair_shape, pair_shape, jax.ShapeDtypeStruct((seqs, 8, inner), jnp.float32)],
        scratch_shapes=[pltpu.VMEM((tokens * groups, 128), jnp.float32)] * 5
        + [pltpu.VMEM((tokens, states, groups, 128), jnp.float32)],
        compiler_params=pltpu.CompilerParams(vmem_limit_bytes=VMEM_LIMIT),
        cost_estimate=pl.CostEstimate(flops=22 * elements, bytes_accessed=24 * raw.size, transcendentals=2 * elements),
        name="scan_both",
    )(raw, conv, gate, gg, skip.reshape(1, inner), a2, h0, q0, b.reshape(-1), c.reshape(-1), cut.reshape(-1))


def pair_sum(value, states):
    total = jnp.sum(value, axis=(0, 2))
    return total.reshape(-1, states)


from jax.sharding import PartitionSpec as P

EPSILON = 1e-05
BF16 = jnp.bfloat16


def from_behind(value, axis, by):
    devices = lax.axis_size(axis)
    pairs = [(i, i + by) for i in range(devices) if 0 <= i + by < devices]
    return lax.ppermute(value, axis, pairs)


def product(left, right, left_dim, right_dim):
    return lax.dot_general(
        left, right, (((left_dim,), (right_dim,)), ((), ())), preferred_element_type=jnp.float32
    )


def exchange_ends(last, total, back, axis):
    devices, here = lax.axis_size(axis), lax.axis_index(axis)
    everything = lax.all_gather(jnp.stack([last, total, back]), axis)
    state = jnp.zeros_like(last)
    for k in range(devices - 1):
        state = jnp.where(k < here, everything[k, 1] * state + everything[k, 0], state)
    adjoint = jnp.zeros_like(last)
    for k in reversed(range(1, devices)):
        adjoint = jnp.where(k > here, everything[k, 1] * adjoint + everything[k, 2], adjoint)
    return state, adjoint


def per_device(
    stream,
    norm_gain,
    in_weight,
    select_weight,
    delta_weight,
    delta_bias,
    out_weight,
    filter_weight,
    filter_bias,
    decay_log,
    skip_gain,
    segments,
    modality,
    valid,
    upstream,
):
    seqs, local_len, part_width = stream.shape
    width = norm_gain.shape[0]
    inner = out_weight.shape[0]
    states = decay_log.shape[0]
    reach = filter_weight.shape[0] - 1
    rows = seqs * local_len
    full_out = lax.all_gather(out_weight, "shard", axis=1, tiled=True)
    full_in = lax.all_gather(in_weight, "shard", axis=1, tiled=True)
    full_select = lax.all_gather(select_weight, "shard", axis=1, tiled=True)
    full_delta = lax.all_gather(delta_weight, "shard", axis=1, tiled=True)
    modes = full_in.shape[0]
    full_in = full_in.reshape(modes, width, 2 * inner)
    rank = full_delta.shape[1]
    mode_rows = modality.reshape(rows)
    masks = jnp.stack([(mode_rows == index).astype(BF16)[:, None] for index in range(modes)])
    masks_float = masks.astype(jnp.float32)
    valid_rows = valid.reshape(rows, 1).astype(jnp.float32)

    def apply_modes(values, weights, weight_dim):
        total = product(values * masks[0], weights[0], 1, weight_dim)
        for index in range(1, modes):
            total = total + product(values * masks[index], weights[index], 1, weight_dim)
        return total

    def modal_terms(values, grads):
        return jnp.stack([product(values * masks[index], grads, 0, 0) for index in range(modes)])

    g_mix = lax.all_gather(upstream, "tp", axis=2, tiled=True).reshape(rows, width) * valid_rows.astype(BF16)
    g_gated = product(g_mix, full_out, 1, 1)

    whole = lax.all_gather(stream, "tp", axis=2, tiled=True).reshape(rows, width).astype(jnp.float32)
    inverse = lax.rsqrt(jnp.mean(whole * whole, axis=1, keepdims=True) + EPSILON)
    normed = (whole * inverse * norm_gain).astype(BF16)
    projected = apply_modes(normed, full_in, 0)
    conv_in = projected[:, :inner].astype(BF16).reshape(seqs, local_len, inner)
    gate_in = projected[:, inner:]
    edge = from_behind(conv_in[:, local_len - reach :], "ctx", 1)
    extended = jnp.concatenate([edge, conv_in], axis=1).astype(jnp.float32)
    offset = lax.axis_index("ctx") * local_len
    padded = jnp.concatenate([jnp.full((seqs, reach), -1, jnp.int32), segments], axis=1)
    seg_ext = lax.dynamic_slice_in_dim(padded, offset, local_len + reach, 1)
    own_seg = seg_ext[:, reach:]
    same = [
        (seg_ext[:, reach - lag : reach - lag + local_len] == own_seg).astype(jnp.float32)[:, :, None]
        for lag in range(reach + 1)
    ]
    taps = [extended[:, reach - lag : reach - lag + local_len] for lag in range(reach + 1)]
    pre = jnp.zeros((seqs, local_len, inner), jnp.float32) + filter_bias
    for lag in range(reach + 1):
        pre = pre + filter_weight[reach - lag] * taps[lag] * same[lag]
    cut = (1.0 - same[1][:, :, 0]) * 1e30
    conv_out = jax.nn.silu(pre).astype(BF16).reshape(rows, inner)
    selected = lax.psum(apply_modes(conv_out, full_select, 1), "tp")
    delta_low = selected[:, :rank].astype(BF16)
    b_in = selected[:, rank : rank + states]
    c_out = selected[:, rank + states :]
    bias_rows = sum(masks_float[index] * delta_bias[index] for index in range(modes))
    raw = apply_modes(delta_low, full_delta, 0) + bias_rows

    neg_decay = -jnp.exp(decay_log)
    _, blocks, groups = sizes(raw, seqs, states)
    a2 = state_form(neg_decay * LOG2E, blocks, groups)
    ends = scan_ends(raw, conv_out, gate_in, g_gated, a2, b_in, c_out, cut, seqs)
    carried, behind = exchange_ends(*ends, "ctx")
    gated, g_gate, g_raw, g_conv, g_neg, g_b, g_c, g_skip = scan_both(
        raw, conv_out, gate_in, g_gated, skip_gain, a2, carried, behind, b_in, c_out, cut, seqs
    )

    out_terms = product(gated, g_mix, 0, 0).astype(BF16)
    out_grad = lax.psum_scatter(out_terms, ("shard", "ctx"), scatter_dimension=1, tiled=True)
    mix_local = (
        lax.psum_scatter(
            product(gated, full_out, 1, 0).astype(BF16), "tp", scatter_dimension=1, tiled=True
        ).astype(jnp.float32)
        * valid_rows
    )
    local_stream = stream.reshape(rows, part_width).astype(jnp.float32)
    output = (local_stream + mix_local).astype(BF16).reshape(seqs, local_len, part_width)
    stream_sq = jnp.sum(valid_rows * local_stream * local_stream)
    mixer_sq = jnp.sum(mix_local * mix_local)
    count = jnp.sum(valid_rows)
    skip_grad = jnp.sum(g_skip, axis=(0, 1))
    decay_grad = from_state_form(jnp.sum(g_neg, axis=0)) * neg_decay
    bias_grad = product(masks[:, :, 0], g_raw, 1, 0)
    delta_terms = modal_terms(delta_low, g_raw)
    g_low = apply_modes(g_raw, full_delta, 1)
    select_part = jnp.concatenate([g_low, pair_sum(g_b, states), pair_sum(g_c, states)], axis=1)
    g_sel_low = lax.psum(select_part, "tp").astype(BF16)
    select_terms = modal_terms(g_sel_low, conv_out)
    g_conv = g_conv + apply_modes(g_sel_low, full_select, 0)
    sig_pre = jax.nn.sigmoid(pre)
    g_pre = g_conv.reshape(seqs, local_len, inner) * sig_pre * (1.0 + pre * (1.0 - sig_pre))
    offset_grad = jnp.sum(g_pre, axis=(0, 1))
    filter_rows = [None] * (reach + 1)
    g_ext = jnp.zeros((seqs, local_len + reach, inner), jnp.float32)
    for lag in range(reach + 1):
        masked = g_pre * same[lag]
        filter_rows[reach - lag] = jnp.sum(masked * taps[lag], axis=(0, 1))
        g_ext = g_ext + jnp.pad(filter_weight[reach - lag] * masked, ((0, 0), (reach - lag, lag), (0, 0)))
    filter_grad = jnp.stack(filter_rows)
    returned = from_behind(g_ext[:, :reach], "ctx", -1)
    g_conv_in = g_ext[:, reach:] + jnp.pad(returned, ((0, 0), (local_len - reach, 0), (0, 0)))
    g_projected = jnp.concatenate([g_conv_in.reshape(rows, inner).astype(BF16), g_gate], axis=1)
    in_terms = modal_terms(normed, g_projected).astype(BF16).reshape(modes, width, 2, inner)
    in_grad = lax.psum_scatter(in_terms, ("shard", "ctx"), scatter_dimension=1, tiled=True)
    select_grad = lax.psum_scatter(select_terms, ("shard", "ctx"), scatter_dimension=1, tiled=True)
    delta_grad = lax.psum_scatter(delta_terms, ("shard", "ctx"), scatter_dimension=1, tiled=True)

    g_normed_part = apply_modes(g_projected, full_in, 1)
    row_part = jnp.sum(g_normed_part * norm_gain * whole, axis=1, keepdims=True)
    row_total = lax.psum(row_part, "tp")
    g_normed = lax.psum_scatter(
        g_normed_part.astype(BF16), "tp", scatter_dimension=1, tiled=True
    ).astype(jnp.float32)
    start = lax.axis_index("tp") * part_width
    own_gain = lax.dynamic_slice_in_dim(norm_gain, start, part_width, 0)
    g_stream = inverse * own_gain * g_normed - local_stream * inverse**3 * row_total / width
    gain_grad = jnp.sum(g_normed * local_stream * inverse, axis=0)
    upstream_local = upstream.reshape(rows, part_width).astype(jnp.float32)
    stream_gradient = (upstream_local + g_stream).astype(BF16).reshape(seqs, local_len, part_width)

    sums = lax.psum(
        (gain_grad, bias_grad, filter_grad, offset_grad, decay_grad, skip_grad, count), ("shard", "ctx")
    )
    squares = lax.psum((stream_sq, mixer_sq), ("shard", "ctx", "tp"))
    denominator = jnp.maximum(sums[6], 1.0) * width
    stream_rms = jnp.sqrt(squares[0] / denominator)
    mixer_rms = jnp.sqrt(squares[1] / denominator)
    return (
        output,
        stream_gradient,
        sums[0],
        in_grad.astype(jnp.float32),
        select_grad,
        delta_grad,
        sums[1],
        out_grad.astype(jnp.float32),
        sums[2],
        sums[3],
        sums[4],
        sums[5],
        stream_rms,
        mixer_rms,
    )


def solution(mesh):
    return jax.shard_map(
        per_device,
        mesh=mesh,
        in_specs=(
            P("shard", "ctx", "tp"),
            P(),
            P(None, "shard", None, "tp"),
            P(None, "shard", "tp"),
            P(None, "shard", "tp"),
            P(None, "tp"),
            P("tp", "shard"),
            P(None, "tp"),
            P("tp"),
            P(None, "tp"),
            P("tp"),
            P("shard", None),
            P("shard", "ctx"),
            P("shard", "ctx"),
            P("shard", "ctx", "tp"),
        ),
        out_specs=(
            P("shard", "ctx", "tp"),
            P("shard", "ctx", "tp"),
            P("tp"),
            P(None, ("shard", "ctx"), None, "tp"),
            P(None, ("shard", "ctx"), "tp"),
            P(None, ("shard", "ctx"), "tp"),
            P(None, "tp"),
            P("tp", ("shard", "ctx")),
            P(None, "tp"),
            P("tp"),
            P(None, "tp"),
            P("tp"),
            P(),
            P(),
        ),
        check_vma=False,
    )
```

```python
import functools
import jax
import jax.numpy as jnp
from jax import lax
from jax.experimental import pallas as pl
from jax.experimental.pallas import tpu as pltpu

LOG2E = 1.4426950408889634
VMEM_LIMIT = 60 * 1024 * 1024


def sigmoid(value):
    return 1.0 / (1.0 + jnp.exp(-value))


def softplus(value):
    return jnp.maximum(value, 0.0) + jnp.log1p(jnp.exp(-jnp.abs(value)))


def stage_rows(raw_ref, conv_ref, gate_ref, gg_ref, delta_s, conv_s, g_s, groups):
    def step(block, _):
        top = pl.multiple_of(block * 16, 16)
        for group in range(groups):
            lanes = slice(group * 128, group * 128 + 128)
            delta = softplus(raw_ref[pl.ds(top, 16), lanes])
            conv = conv_ref[pl.ds(top, 16), lanes].astype(jnp.float32)
            gate = gate_ref[pl.ds(top, 16), lanes]
            g_mixed = gg_ref[pl.ds(top, 16), lanes] * (gate * sigmoid(gate))
            for part in range(2):
                rows = pl.ds(pl.multiple_of(((block * 2 + part) * groups + group) * 8, 8), 8)
                eight = slice(part * 8, part * 8 + 8)
                delta_s[rows, :] = delta[eight]
                conv_s[rows, :] = conv[eight]
                g_s[rows, :] = g_mixed[eight]
        return 0

    lax.fori_loop(0, raw_ref.shape[0] // 16, step, 0)


def ends_kernel(groups, states, split, raw_ref, conv_ref, gate_ref, gg_ref, a_ref, b_ref, c_ref,
                cut_ref, h_ref, p_ref, l_ref, delta_s, conv_s, g_s):
    tokens = raw_ref.shape[0]
    first = pl.program_id(0) * tokens
    stage_rows(raw_ref, conv_ref, gate_ref, gg_ref, delta_s, conv_s, g_s, groups)
    for low in range(0, states, split):
        names = range(low, low + split)

        def eight_tokens(tile, carry):
            h, p, l = (list(part) for part in carry)
            for i in range(8):
                rows = pl.ds(tile * (groups * 8) + i, groups, stride=8)
                delta = delta_s[rows, :]
                signal = delta * conv_s[rows, :]
                g = g_s[rows, :]
                token = first + tile * 8 + i
                reach = delta + cut_ref[token]
                for k, n in enumerate(names):
                    decay = jnp.exp2(reach * a_ref[n])
                    h[k] = decay * h[k] + signal * b_ref[token * states + n]
                    p[k] = decay * p[k]
                    l[k] = l[k] + p[k] * (g * c_ref[token * states + n])
            return tuple(h), tuple(p), tuple(l)

        zero = tuple(jnp.zeros((groups, 128), jnp.float32) for _ in names)
        one = tuple(jnp.ones((groups, 128), jnp.float32) for _ in names)
        h, p, l = lax.fori_loop(0, tokens // 8, eight_tokens, (zero, one, zero))
        for k, n in enumerate(names):
            h_ref[n], p_ref[n], l_ref[n] = h[k], p[k], l[k]


def scan_kernel(groups, states, fsplit, bsplit, raw_ref, conv_ref, gate_ref, gg_ref, skip_ref, a_ref, h0_ref,
                q0_ref, b_ref, c_ref, cut_ref, gated_ref, ggate_ref, graw_ref, gconv_ref,
                ga_ref, gb_ref, gc_ref, gskip_ref, delta_s, conv_s, g_s, y_s, gs_s, h_s):
    tokens = raw_ref.shape[0]
    tiles = tokens // 8
    first = pl.program_id(0) * tokens
    stage_rows(raw_ref, conv_ref, gate_ref, gg_ref, delta_s, conv_s, g_s, groups)
    lane = lax.broadcasted_iota(jnp.int32, (groups, 128), 1)

    def split_sum(total, names, values, i):
        for n, value in zip(names, values):
            total = jnp.where(lane == i * states + n, jnp.sum(value, axis=1, keepdims=True), total)
        return total

    for low in range(0, states, fsplit):
        names = range(low, low + fsplit)

        def forward(tile, h):
            h = list(h)
            gc = jnp.zeros((groups, 128), jnp.float32) if low == 0 else gc_ref[tile]
            for i in range(8):
                rows = pl.ds(tile * (groups * 8) + i, groups, stride=8)
                delta = delta_s[rows, :]
                signal = delta * conv_s[rows, :]
                g = g_s[rows, :]
                token = tile * 8 + i
                at = (first + token) * states
                reach = delta + cut_ref[first + token]
                y = None
                parts = []
                for k, n in enumerate(names):
                    h_s[token, n] = h[k]
                    decay = jnp.exp2(reach * a_ref[n])
                    h[k] = decay * h[k] + signal * b_ref[at + n]
                    term = h[k] * c_ref[at + n]
                    y = term if y is None else y + term
                    parts.append(h[k] * g)
                gc = split_sum(gc, names, parts, i)
                y_s[rows, :] = y if low == 0 else y + y_s[rows, :]
            gc_ref[tile] = gc
            return tuple(h)

        lax.fori_loop(0, tiles, forward, tuple(h0_ref[n] for n in names))

    def between(block, total):
        top = pl.multiple_of(block * 16, 16)
        new = []
        for group in range(groups):
            lanes = slice(group * 128, group * 128 + 128)
            gate = gate_ref[pl.ds(top, 16), lanes]
            sig = sigmoid(gate)
            y, conv, g = (
                jnp.concatenate([ref[pl.ds(pl.multiple_of(((block * 2 + part) * groups + group) * 8, 8), 8), :]
                                 for part in range(2)], axis=0)
                for ref in (y_s, conv_s, g_s)
            )
            mixed = y + skip_ref[:, lanes] * conv
            gated_ref[pl.ds(top, 16), lanes] = (mixed * (gate * sig)).astype(jnp.bfloat16)
            g_gate = gg_ref[pl.ds(top, 16), lanes] * mixed * sig * (1.0 + gate * (1.0 - sig))
            ggate_ref[pl.ds(top, 16), lanes] = g_gate.astype(jnp.bfloat16)
            product = g * conv
            new.append(total[group] + product[:8] + product[8:])
        return tuple(new)

    sums = lax.fori_loop(0, tokens // 16, between,
                         tuple(jnp.zeros((8, 128), jnp.float32) for _ in range(groups)))
    for group in range(groups):
        gskip_ref[:, group * 128:group * 128 + 128] = sums[group]

    for low in range(0, states, bsplit):
        names = range(low, low + bsplit)

        def backward(step, carry):
            q, ga = (list(part) for part in carry)
            tile = tiles - 1 - step
            gb = jnp.zeros((groups, 128), jnp.float32) if low == 0 else gb_ref[tile]
            for i in reversed(range(8)):
                rows = pl.ds(tile * (groups * 8) + i, groups, stride=8)
                delta = delta_s[rows, :]
                conv = conv_s[rows, :]
                signal = delta * conv
                g = g_s[rows, :]
                token = tile * 8 + i
                at = (first + token) * states
                reach = delta + cut_ref[first + token]
                gd = gs = None
                parts = []
                for k, n in enumerate(names):
                    decay = jnp.exp2(reach * a_ref[n])
                    lam = q[k] + g * c_ref[at + n]
                    q[k] = decay * lam
                    w = q[k] * h_s[token, n]
                    ga[k] = ga[k] + w * delta
                    d_term = w * a_ref[n]
                    s_term = lam * b_ref[at + n]
                    gd = d_term if gd is None else gd + d_term
                    gs = s_term if gs is None else gs + s_term
                    parts.append(lam * signal)
                gb = split_sum(gb, names, parts, i)
                y_s[rows, :] = gd if low == 0 else gd + y_s[rows, :]
                gs_s[rows, :] = gs if low == 0 else gs + gs_s[rows, :]
            gb_ref[tile] = gb
            return tuple(q), tuple(ga)

        zero = tuple(jnp.zeros((groups, 128), jnp.float32) for _ in names)
        _, ga = lax.fori_loop(0, tiles, backward, (tuple(q0_ref[n] for n in names), zero))
        for k, n in enumerate(names):
            ga_ref[n] = ga[k]

    def after(block, _):
        top = pl.multiple_of(block * 16, 16)
        for group in range(groups):
            lanes = slice(group * 128, group * 128 + 128)
            raw = raw_ref[pl.ds(top, 16), lanes]
            gd, gs, conv, delta, g = (
                jnp.concatenate([ref[pl.ds(pl.multiple_of(((block * 2 + part) * groups + group) * 8, 8), 8), :]
                                 for part in range(2)], axis=0)
                for ref in (y_s, gs_s, conv_s, delta_s, g_s)
            )
            g_delta = gd * (1.0 / LOG2E) + conv * gs
            graw_ref[pl.ds(top, 16), lanes] = (g_delta * sigmoid(raw)).astype(jnp.bfloat16)
            gconv_ref[pl.ds(top, 16), lanes] = skip_ref[:, lanes] * g + delta * gs
        return 0

    lax.fori_loop(0, tokens // 16, after, 0)


def sizes(raw, seqs, states):
    rows, inner = raw.shape
    groups = min(8, inner // 128)
    return rows // seqs, inner // (groups * 128), groups


def state_form(value, blocks, groups):
    states = value.shape[0]
    return value.reshape(states, blocks, groups, 128).transpose(1, 0, 2, 3)


def from_state_form(value):
    blocks, states, groups, lanes = value.shape
    return value.transpose(1, 0, 2, 3).reshape(states, blocks * groups * lanes)


def token_spec(tokens, width, block):
    return pl.BlockSpec((tokens, width), lambda s: (s, block))


def state_spec(states, groups):
    return pl.BlockSpec((None, states, groups, 128), lambda s: (s, 0, 0, 0))


def scan_ends(raw, conv, gate, gg, a2, b, c, cut, seqs, block):
    states, groups, _ = a2.shape
    tokens = raw.shape[0] // seqs
    width = groups * 128
    smem = pl.BlockSpec(memory_space=pltpu.SMEM)
    out = jax.ShapeDtypeStruct((seqs, states, groups, 128), jnp.float32)
    elements = raw.shape[0] * width * states
    return pl.pallas_call(
        functools.partial(ends_kernel, groups, states, states),
        grid=(seqs,),
        in_specs=[token_spec(tokens, width, block)] * 4
        + [pl.BlockSpec((states, groups, 128), lambda s: (0, 0, 0)), smem, smem, smem],
        out_specs=[state_spec(states, groups)] * 3,
        out_shape=[out] * 3,
        scratch_shapes=[pltpu.VMEM((tokens * groups, 128), jnp.float32)] * 3,
        compiler_params=pltpu.CompilerParams(vmem_limit_bytes=VMEM_LIMIT),
        cost_estimate=pl.CostEstimate(flops=8 * elements, bytes_accessed=elements, transcendentals=elements),
        name="scan_ends",
    )(raw, conv, gate, gg, a2, b.reshape(-1), c.reshape(-1), cut.reshape(-1))


def scan_both(raw, conv, gate, gg, skip, a2, h0, q0, b, c, cut, seqs, block):
    states, groups, _ = a2.shape
    rows, inner = raw.shape
    tokens = rows // seqs
    width = groups * 128
    smem = pl.BlockSpec(memory_space=pltpu.SMEM)
    elements = rows * width * states
    token = token_spec(tokens, width, block)
    tiles = tokens // 8
    own = pl.BlockSpec((tokens, width), lambda s: (s, 0))
    pair = pl.BlockSpec((tiles, groups, 128), lambda s: (s, 0, 0))
    pair_shape = jax.ShapeDtypeStruct((rows // 8, groups, 128), jnp.float32)
    low = jax.ShapeDtypeStruct((rows, width), jnp.bfloat16)
    return pl.pallas_call(
        functools.partial(scan_kernel, groups, states, states, states),
        grid=(seqs,),
        in_specs=[token] * 4
        + [pl.BlockSpec((1, width), lambda s: (0, block)),
           pl.BlockSpec((states, groups, 128), lambda s: (0, 0, 0)),
           state_spec(states, groups), state_spec(states, groups), smem, smem, smem],
        out_specs=[own] * 4 + [state_spec(states, groups), pair, pair,
                               pl.BlockSpec((None, 8, width), lambda s: (s, 0, 0))],
        out_shape=[low, low, low, jax.ShapeDtypeStruct((rows, width), jnp.float32),
                   jax.ShapeDtypeStruct((seqs, states, groups, 128), jnp.float32),
                   pair_shape, pair_shape, jax.ShapeDtypeStruct((seqs, 8, width), jnp.float32)],
        scratch_shapes=[pltpu.VMEM((tokens * groups, 128), jnp.float32)] * 5
        + [pltpu.VMEM((tokens, states, groups, 128), jnp.float32)],
        compiler_params=pltpu.CompilerParams(vmem_limit_bytes=VMEM_LIMIT),
        cost_estimate=pl.CostEstimate(flops=22 * elements, bytes_accessed=2 * elements, transcendentals=2 * elements),
        name="scan_both",
    )(raw, conv, gate, gg, skip.reshape(1, inner), a2, h0, q0, b.reshape(-1), c.reshape(-1), cut.reshape(-1))


def pair_sum(value, states):
    return jnp.sum(value, axis=1).reshape(-1, states)


MESH = pl.DeviceIdType.MESH


def gather_kernel(chunks, conv_ref, gate_ref, out_ref, conv_full, gate_full, out_full, local_sem, core_send,
                  core_recv, y_send, y_recv, z_send, z_recv, pass_send, pass_recv, rest_send, rest_recv):
    shard, ctx = lax.axis_index("shard"), lax.axis_index("ctx")
    mine, far = shard, lax.rem(shard + 2, 4)
    core = {"shard": shard + 1 - 2 * lax.rem(shard, 2)}
    across = {"shard": far}
    side = {"ctx": ctx + 1 - 2 * lax.rem(ctx, 2)}
    half = lax.rem(ctx, 2)
    depth = conv_ref.shape[1]
    columns = out_ref.shape[1]
    piece = depth // 2 // chunks
    piece_out = out_ref.shape[0] // 2 // chunks

    barrier = pltpu.get_barrier_semaphore()
    for peer in (core, across, side):
        pl.semaphore_signal(barrier, inc=1, device_id=peer, device_id_type=MESH)
    pl.semaphore_wait(barrier, 3)

    def views(owner, part, i):
        rows = pl.ds(pl.multiple_of(owner * depth + (part * chunks + i) * piece, piece), piece)
        tall = pl.ds(pl.multiple_of((part * chunks + i) * piece_out, piece_out), piece_out)
        wide = pl.ds(pl.multiple_of(owner * columns, columns), columns)
        return conv_full.at[:, rows], gate_full.at[:, rows], out_full.at[tall, wide]

    def own(part, i):
        rows = pl.ds(pl.multiple_of((part * chunks + i) * piece, piece), piece)
        tall = pl.ds(pl.multiple_of((part * chunks + i) * piece_out, piece_out), piece_out)
        return conv_ref.at[:, rows], gate_ref.at[:, rows], out_ref.at[tall, :]

    def send(source, target, to, send_sem, recv_sem):
        copies = [
            pltpu.make_async_remote_copy(src_ref=s, dst_ref=t, send_sem=send_sem.at[k], recv_sem=recv_sem.at[k],
                                         device_id=to, device_id_type=MESH)
            for k, (s, t) in enumerate(zip(source, target))
        ]
        for copy in copies:
            copy.start()
        return copies

    def cross(i):
        return send(own(half, i), views(mine, half, i), across, y_send.at[i], y_recv.at[i])

    to_far = [cross(i) for i in range(min(2, chunks))]
    rows = pl.ds(pl.multiple_of(mine * depth, depth), depth)
    wide = pl.ds(pl.multiple_of(mine * columns, columns), columns)
    source = (conv_ref, gate_ref, out_ref)
    place = (conv_full.at[:, rows], gate_full.at[:, rows], out_full.at[:, wide])
    stay = [pltpu.make_async_copy(s, t, local_sem.at[k]) for k, (s, t) in enumerate(zip(source, place))]
    for copy in stay:
        copy.start()
    to_core = send(source, place, core, core_send, core_recv)
    onward = []
    for i in range(chunks):
        for copy in to_far[i]:
            copy.wait()
        if i + 2 < chunks:
            to_far.append(cross(i + 2))
        held = views(far, half, i)
        onward.append(send(held, held, side, z_send.at[i], z_recv.at[i]))
        to_core += send(held, held, core, pass_send.at[i], pass_recv.at[i])
    for i in range(chunks):
        for copy in onward[i]:
            copy.wait_recv()
        held = views(far, 1 - half, i)
        to_core += send(held, held, core, rest_send.at[i], rest_recv.at[i])
    for copy in stay:
        copy.wait()
    for copy in to_core:
        copy.wait()
    for i in range(chunks):
        for copy in onward[i]:
            copy.wait_send()


def gather_weights(in_own, out_own, chunks=8):
    _, modes, depth, inner = in_own.shape
    any_space = pl.BlockSpec(memory_space=pl.ANY)
    vmem = pl.BlockSpec(memory_space=pltpu.VMEM)
    many = pltpu.SemaphoreType.DMA((chunks, 3))
    three = pltpu.SemaphoreType.DMA((3,))
    full = jax.ShapeDtypeStruct((modes, 4 * depth, inner), in_own.dtype)
    return pl.pallas_call(
        functools.partial(gather_kernel, chunks),
        in_specs=[vmem] * 3,
        out_specs=[any_space] * 3,
        out_shape=[full, full, jax.ShapeDtypeStruct((inner, 4 * out_own.shape[1]), out_own.dtype)],
        scratch_shapes=[three] * 3 + [many] * 8,
        compiler_params=pltpu.CompilerParams(collective_id=1, has_side_effects=True, vmem_limit_bytes=32 * 2**20),
        cost_estimate=pl.CostEstimate(flops=0, bytes_accessed=400_000_000, transcendentals=0),
        name="gather_weights",
    )(in_own[0], in_own[1], out_own)


def finish_kernel(x_ref, gate_ref, conv_ref, gated_ref, sum_ref, blocks, part, below, above, y_send, y_recv,
                  core_send, core_recv, pass_send, pass_recv, local_sem, up_send, up_recv, down_send, down_recv):
    shard, ctx = lax.axis_index("shard"), lax.axis_index("ctx")
    far = lax.rem(shard + 2, 4)
    core = {"shard": shard + 1 - 2 * lax.rem(shard, 2)}
    across = {"shard": far}
    jobs, units, last = blocks.shape[0], part.shape[0], 3
    tokens, width = gate_ref.shape
    deep = sum_ref.shape[1]
    up, down = {"ctx": ctx + 1}, {"ctx": ctx - 1}

    barrier = pltpu.get_barrier_semaphore()
    for peer in (core, across):
        pl.semaphore_signal(barrier, inc=1, device_id=peer, device_id_type=MESH)

    @pl.when(ctx < last)
    def _():
        pl.semaphore_signal(barrier, inc=1, device_id=up, device_id_type=MESH)

    @pl.when(ctx > 0)
    def _():
        pl.semaphore_signal(barrier, inc=1, device_id=down, device_id_type=MESH)

    pl.semaphore_wait(barrier, 2 + jnp.where(ctx < last, 1, 0) + jnp.where(ctx > 0, 1, 0))

    sources = [gate_ref, conv_ref.at[:, pl.ds(0, width)], conv_ref.at[:, pl.ds(width, width)], gated_ref]

    def rows_of(owner):
        return pl.ds(pl.multiple_of(owner * tokens, tokens), tokens)

    def remote(source, target, send_sem, recv_sem, to):
        return pltpu.make_async_remote_copy(src_ref=source, dst_ref=target, send_sem=send_sem, recv_sem=recv_sem,
                                            device_id=to, device_id_type=MESH)

    def cross(j):
        return remote(sources[j], blocks.at[j, rows_of(shard)], y_send.at[j], y_recv.at[j], across)

    def pair(j):
        return remote(sources[j], blocks.at[j, rows_of(shard)], core_send.at[j], core_recv.at[j], core)

    def onward(j):
        held = blocks.at[j, rows_of(far)]
        return remote(held, held, pass_send.at[j], pass_recv.at[j], core)

    def stay(j):
        return pltpu.make_async_copy(sources[j], blocks.at[j, rows_of(shard)], local_sem.at[j])

    def advance(j):
        cross(j).wait()
        onward(j).start()
        if j + 2 < jobs:
            cross(j + 2).start()

    def hop(u, k, buffer, send_sem, recv_sem, to):
        rows = pl.ds(pl.multiple_of(k * deep, deep), deep)
        return remote(part.at[u, rows], buffer.at[u, rows], send_sem.at[u, k], recv_sem.at[u, k], to)

    def going_up(u, k):
        return hop(u, k, below, up_send, up_recv, up)

    def going_down(u, k):
        return hop(u, k, above, down_send, down_recv, down)

    def add(u, k, buffer):
        rows = pl.ds(k * deep, deep)
        total = part[u, rows, :].astype(jnp.float32) + buffer[u, rows, :].astype(jnp.float32)
        part[u, rows, :] = total.astype(part.dtype)

    for j in range(min(2, jobs)):
        cross(j).start()
    for j in range(jobs):
        stay(j).start()
        pair(j).start()
    advance(0)

    def step(t, _):
        for j in range(jobs):
            @pl.when(t == 2 * j)
            def _():
                stay(j).wait()
                pair(j).wait()
                onward(j).wait()

        @pl.when(t < units)
        def _():
            job = t // 2
            which = jnp.where(t == 2 * (jobs - 1), 2, lax.rem(t, 2))
            for c in range(width // 256):
                lanes = slice(c * 256, c * 256 + 256)
                part[t, :, lanes] = jnp.dot(
                    x_ref[which], blocks[job, :, lanes], preferred_element_type=jnp.float32
                ).astype(part.dtype)

        u = t - ctx

        @pl.when((u >= 0) & (u < units))
        def _():
            for k in range(last, 0, -1):
                @pl.when(k > ctx)
                def _():
                    @pl.when(ctx > 0)
                    def _():
                        going_up(u, k).wait_recv()
                        add(u, k, below)

                    going_up(u, k).start()

        v = t - (last - ctx)

        @pl.when((v >= 0) & (v < units))
        def _():
            for k in range(last):
                @pl.when(k < ctx)
                def _():
                    @pl.when(ctx < last)
                    def _():
                        going_down(v, k).wait_recv()
                        add(v, k, above)

                    going_down(v, k).start()

        w = t - last

        @pl.when(w >= 0)
        def _():
            rows = pl.ds(pl.multiple_of(ctx * deep, deep), deep)
            sum_ref[w] = part[w, rows, :].astype(jnp.float32)

            @pl.when(ctx > 0)
            def _():
                going_up(w, ctx).wait_recv()
                sum_ref[w] += below[w, rows, :].astype(jnp.float32)

            @pl.when(ctx < last)
            def _():
                going_down(w, ctx).wait_recv()
                sum_ref[w] += above[w, rows, :].astype(jnp.float32)

        for j in range(1, jobs):
            @pl.when(t == 2 * j - 1)
            def _():
                advance(j)

        return 0

    lax.fori_loop(0, units + last, step, 0)

    def drain(u, _):
        for k in range(last + 1):
            @pl.when(k > ctx)
            def _():
                going_up(u, k).wait_send()

            @pl.when(k < ctx)
            def _():
                going_down(u, k).wait_send()

        return 0

    lax.fori_loop(0, units, drain, 0)


def finish_weights(x, g_gate, g_conv_in, gated):
    _, features, group = x.shape
    tokens, width = g_gate.shape
    jobs, units = 4, 7
    deep = features // 4
    any_space = pl.BlockSpec(memory_space=pl.ANY)
    vmem = pl.BlockSpec(memory_space=pltpu.VMEM)
    sums = pltpu.SemaphoreType.DMA((units, 4))
    job_sems = pltpu.SemaphoreType.DMA((jobs,))
    flops = 2 * units * features * group * width
    return pl.pallas_call(
        finish_kernel,
        in_specs=[vmem, any_space, any_space, any_space],
        out_specs=vmem,
        out_shape=jax.ShapeDtypeStruct((units, deep, width), jnp.float32),
        scratch_shapes=[pltpu.VMEM((jobs, group, width), jnp.bfloat16)]
        + [pltpu.VMEM((units, features, width), jnp.bfloat16)] * 3
        + [job_sems] * 7 + [sums] * 4,
        compiler_params=pltpu.CompilerParams(collective_id=2, has_side_effects=True, vmem_limit_bytes=VMEM_LIMIT),
        cost_estimate=pl.CostEstimate(flops=flops, bytes_accessed=500_000_000, transcendentals=0),
        name="finish_weights",
    )(x, g_gate, g_conv_in, gated)


def small_kernel(in_ref, out_ref, x_in, mine, y_in, z_in, x_sem, a_send, a_recv, b_send, b_recv, c_send, c_recv):
    shard, ctx, tp = lax.axis_index("shard"), lax.axis_index("ctx"), lax.axis_index("tp")
    quarter = out_ref.shape[0] // 4
    other = {"tp": 1 - tp}

    def shard_peer(k):
        return {"shard": lax.rem(shard + k, 4)}

    def ctx_peer(k):
        return {"ctx": lax.rem(ctx + k, 4)}

    barrier = pltpu.get_barrier_semaphore()
    pl.semaphore_signal(barrier, inc=1, device_id=other, device_id_type=MESH)
    for k in range(1, 4):
        pl.semaphore_signal(barrier, inc=1, device_id=shard_peer(k), device_id_type=MESH)
        pl.semaphore_signal(barrier, inc=1, device_id=ctx_peer(k), device_id_type=MESH)
    pl.semaphore_wait(barrier, 7)

    def remote(source, target, send_sem, recv_sem, to):
        copy = pltpu.make_async_remote_copy(src_ref=source, dst_ref=target, send_sem=send_sem, recv_sem=recv_sem,
                                            device_id=to, device_id_type=MESH)
        copy.start()
        return copy

    def rows_of(k):
        return pl.ds(pl.multiple_of(k * quarter, 8), quarter)

    total = in_ref.shape[0]
    copy = remote(in_ref.at[pl.ds(total - 8, 8)], x_in, x_sem.at[0], x_sem.at[1], other)
    mine[...] = in_ref[...]
    copy.wait()
    mine[total - 8 :, :] = in_ref[total - 8 :, :] + x_in[...]

    copies = [remote(mine.at[rows_of(lax.rem(shard + k, 4))], y_in.at[k - 1], a_send.at[k - 1], a_recv.at[k - 1],
                     shard_peer(k)) for k in range(1, 4)]
    for copy in copies:
        copy.wait()
    z_in[ctx] = mine[rows_of(shard), :] + y_in[0] + y_in[1] + y_in[2]
    copies = [remote(z_in.at[ctx], z_in.at[ctx], b_send.at[k - 1], b_recv.at[k - 1], ctx_peer(k))
              for k in range(1, 4)]
    for copy in copies:
        copy.wait()
    out_ref[rows_of(shard), :] = (z_in[0] + z_in[1]) + (z_in[2] + z_in[3])
    copies = [remote(out_ref.at[rows_of(shard)], out_ref.at[rows_of(shard)], c_send.at[k - 1], c_recv.at[k - 1],
                     shard_peer(k)) for k in range(1, 4)]
    for copy in copies:
        copy.wait()


def small_sum(value):
    rows, width = value.shape
    quarter = rows // 4
    vmem = pl.BlockSpec(memory_space=pltpu.VMEM)
    three = pltpu.SemaphoreType.DMA((3,))
    return pl.pallas_call(
        small_kernel,
        in_specs=[vmem],
        out_specs=vmem,
        out_shape=jax.ShapeDtypeStruct(value.shape, value.dtype),
        scratch_shapes=[pltpu.VMEM((8, width), value.dtype), pltpu.VMEM(value.shape, value.dtype),
                        pltpu.VMEM((3, quarter, width), value.dtype), pltpu.VMEM((4, quarter, width), value.dtype),
                        pltpu.SemaphoreType.DMA((2,))] + [three] * 6,
        compiler_params=pltpu.CompilerParams(collective_id=3, has_side_effects=True, vmem_limit_bytes=32 * 2**20),
        cost_estimate=pl.CostEstimate(flops=0, bytes_accessed=40_000_000, transcendentals=0),
        name="small_sum",
    )(value)


from jax.sharding import PartitionSpec as P

EPSILON = 1e-05
BF16 = jnp.bfloat16


def from_behind(value, axis, by):
    devices = lax.axis_size(axis)
    pairs = [(i, i + by) for i in range(devices) if 0 <= i + by < devices]
    return lax.ppermute(value, axis, pairs)


def product(left, right, left_dim, right_dim):
    return lax.dot_general(
        left, right, (((left_dim,), (right_dim,)), ((), ())), preferred_element_type=jnp.float32
    )


def exchange_ends(last, total, back, axis):
    devices = lax.axis_size(axis)
    state, adjoint = jnp.zeros_like(last), jnp.zeros_like(last)
    ahead = jnp.stack([last, total]).astype(BF16)
    behind = jnp.stack([back, total]).astype(BF16)
    before = [from_behind(ahead, axis, k) for k in range(1, devices)]
    after = [from_behind(behind, axis, -k) for k in range(1, devices)]
    for part in reversed(before):
        state = part[1].astype(jnp.float32) * state + part[0].astype(jnp.float32)
    for part in reversed(after):
        adjoint = part[1].astype(jnp.float32) * adjoint + part[0].astype(jnp.float32)
    return state, adjoint


def group_rows(normed, g_mix, masks, fast):
    modes, tokens = masks.shape
    count = lax.axis_size("shard")
    width = normed.shape[1]
    deep = width // count
    if not fast:
        both = lax.all_to_all(jnp.stack([normed, g_mix]), "shard", 2, 1, tiled=True)
        flags = lax.all_gather(masks, "shard", axis=1, tiled=True)
        return jnp.stack([(both[0] * flags[index][:, None]).T for index in range(modes)] + [both[1].T])
    flags = jnp.broadcast_to(jnp.pad(masks, ((0, 16 - modes), (0, 0))), (count, 16, tokens))
    bundle = jnp.concatenate(
        [normed.T.reshape(count, deep, tokens), g_mix.T.reshape(count, deep, tokens), flags], axis=1
    )
    here = lax.axis_index("shard")
    whole = jnp.zeros((2 * deep + 16, count * tokens), BF16)
    for k in range(count):
        piece = lax.dynamic_index_in_dim(bundle, here ^ k, 0, keepdims=False)
        if k:
            piece = lax.ppermute(piece, "shard", [(i, i ^ k) for i in range(count)])
        whole = lax.dynamic_update_slice(whole, piece, (0, (here ^ k) * tokens))
    flags = whole[2 * deep :]
    return jnp.stack(
        [whole[:deep] * flags[index : index + 1] for index in range(modes)] + [whole[deep : 2 * deep]]
    )


def per_device(
    stream,
    norm_gain,
    in_weight,
    select_weight,
    delta_weight,
    delta_bias,
    out_weight,
    filter_weight,
    filter_bias,
    decay_log,
    skip_gain,
    segments,
    modality,
    valid,
    upstream,
):
    seqs, local_len, part_width = stream.shape
    width = norm_gain.shape[0]
    inner = out_weight.shape[0]
    states = decay_log.shape[0]
    reach = filter_weight.shape[0] - 1
    rows = seqs * local_len
    tps = lax.axis_size("tp")
    modes, depth = in_weight.shape[:2]
    in_own = in_weight.transpose(2, 0, 1, 3)
    fast = (lax.axis_size("shard"), lax.axis_size("ctx"), lax.axis_size("tp")) == (4, 4, 2)
    if fast:
        conv_weight, gate_weight, full_out = gather_weights(in_own, out_weight)
    else:
        conv_weight, gate_weight = lax.all_gather(in_own, "shard", axis=2, tiled=True)
        full_out = lax.all_gather(out_weight, "shard", axis=1, tiled=True)
    full_select = lax.all_gather(select_weight, "shard", axis=1, tiled=True)
    full_delta = lax.all_gather(delta_weight, "shard", axis=1, tiled=True)
    rank = full_delta.shape[1]
    mode_rows = modality.reshape(rows)
    masks = jnp.stack([(mode_rows == index).astype(BF16)[:, None] for index in range(modes)])
    masks_float = masks.astype(jnp.float32)
    valid_rows = valid.reshape(rows, 1).astype(jnp.float32)

    def apply_modes(values, weights, weight_dim):
        total = product(values * masks[0], weights[0], 1, weight_dim)
        for index in range(1, modes):
            total = total + product(values * masks[index], weights[index], 1, weight_dim)
        return total

    def modal_terms(values, grads):
        return jnp.stack([product(values * masks[index], grads, 0, 0) for index in range(modes)])

    g_mix = lax.all_gather(upstream, "tp", axis=2, tiled=True).reshape(rows, width) * valid_rows.astype(BF16)
    g_gated = product(g_mix, full_out, 1, 1)

    whole = lax.all_gather(stream, "tp", axis=2, tiled=True).reshape(rows, width).astype(jnp.float32)
    inverse = lax.rsqrt(jnp.mean(whole * whole, axis=1, keepdims=True) + EPSILON)
    normed = (whole * inverse * norm_gain).astype(BF16)
    normed_modes = jnp.concatenate([normed * masks[index] for index in range(modes)], axis=1)
    conv_in = product(normed_modes, conv_weight.reshape(modes * width, inner), 1, 0)
    conv_in = conv_in.astype(BF16).reshape(seqs, local_len, inner)
    gate_in = product(normed_modes, gate_weight.reshape(modes * width, inner), 1, 0)
    x = group_rows(normed, g_mix, masks[:, :, 0], fast)

    def terms_of(lefts, grads):
        return jnp.stack([product(left, grads, 1, 0) for left in lefts]).astype(BF16)

    def summed(terms):
        return lax.psum_scatter(terms, "ctx", scatter_dimension=1, tiled=True).astype(jnp.float32)

    edge = from_behind(conv_in[:, local_len - reach :], "ctx", 1)
    extended = jnp.concatenate([edge, conv_in], axis=1).astype(jnp.float32)
    offset = lax.axis_index("ctx") * local_len
    padded = jnp.concatenate([jnp.full((seqs, reach), -1, jnp.int32), segments], axis=1)
    seg_ext = lax.dynamic_slice_in_dim(padded, offset, local_len + reach, 1)
    own_seg = seg_ext[:, reach:]
    same = [
        (seg_ext[:, reach - lag : reach - lag + local_len] == own_seg).astype(jnp.float32)[:, :, None]
        for lag in range(reach + 1)
    ]
    taps = [extended[:, reach - lag : reach - lag + local_len] for lag in range(reach + 1)]
    pre = jnp.zeros((seqs, local_len, inner), jnp.float32) + filter_bias
    for lag in range(reach + 1):
        pre = pre + filter_weight[reach - lag] * taps[lag] * same[lag]
    cut = (1.0 - same[1][:, :, 0]) * 1e30
    conv_out = jax.nn.silu(pre).astype(BF16).reshape(rows, inner)
    selected = lax.psum(apply_modes(conv_out, full_select, 1), "tp")
    delta_low = selected[:, :rank].astype(BF16)
    b_in = selected[:, rank : rank + states]
    c_out = selected[:, rank + states :]
    bias_rows = sum(masks_float[index] * delta_bias[index] for index in range(modes))
    raw = apply_modes(delta_low, full_delta, 0) + bias_rows

    neg_decay = -jnp.exp(decay_log)
    _, blocks, groups = sizes(raw, seqs, states)
    a2 = state_form(neg_decay * LOG2E, blocks, groups)
    ends = [scan_ends(raw, conv_out, gate_in, g_gated, a2[j], b_in, c_out, cut, seqs, j) for j in range(blocks)]
    entering = [exchange_ends(*part, "ctx") for part in ends]
    entering[0], ends[-1], x = lax.optimization_barrier((entering[0], ends[-1], x))
    results = [
        scan_both(raw, conv_out, gate_in, g_gated, skip_gain, a2[j], *entering[j], b_in, c_out, cut, seqs, j)
        for j in range(blocks)
    ]
    early = []
    for part in results[: 1 if fast else blocks]:
        gate_all = lax.all_gather(part[1], "shard", axis=0, tiled=True)
        gated_all = lax.all_gather(part[0], "shard", axis=0, tiled=True)
        early.append((terms_of(x[:modes], gate_all), terms_of(x[modes:], gated_all)))
    early, results = lax.optimization_barrier((early, results))
    gate_grads = [summed(part[0]) for part in early]
    out_grads = [summed(part[1])[0] for part in early]
    gated, g_gate, g_raw, g_conv, g_neg, g_b, g_c, g_skip = zip(*results)
    gated, g_gate, g_raw, g_conv = (jnp.concatenate(part, axis=1) for part in (gated, g_gate, g_raw, g_conv))
    g_skip = jnp.concatenate(g_skip, axis=2)
    g_neg = jnp.stack([jnp.sum(part, axis=0) for part in g_neg])

    mix_local = (
        lax.psum_scatter(
            product(gated, full_out, 1, 0).astype(BF16), "tp", scatter_dimension=1, tiled=True
        ).astype(jnp.float32)
        * valid_rows
    )
    local_stream = stream.reshape(rows, part_width).astype(jnp.float32)
    output = (local_stream + mix_local).astype(BF16).reshape(seqs, local_len, part_width)
    stream_sq = jnp.sum(valid_rows * jnp.sum(whole * whole, axis=1, keepdims=True))
    count = jnp.sum(valid_rows)
    skip_grad = jnp.sum(g_skip, axis=(0, 1))
    decay_grad = from_state_form(g_neg) * neg_decay
    bias_grad = product(masks[:, :, 0], g_raw, 1, 0)
    delta_terms = modal_terms(delta_low, g_raw)
    g_low = apply_modes(g_raw, full_delta, 1)
    select_part = jnp.concatenate([g_low, pair_sum(sum(g_b), states), pair_sum(sum(g_c), states)], axis=1)
    g_sel_low = lax.psum(select_part, "tp").astype(BF16)
    select_terms = modal_terms(g_sel_low, conv_out)
    g_conv = g_conv + apply_modes(g_sel_low, full_select, 0)
    sig_pre = jax.nn.sigmoid(pre)
    g_pre = g_conv.reshape(seqs, local_len, inner) * sig_pre * (1.0 + pre * (1.0 - sig_pre))
    offset_grad = jnp.sum(g_pre, axis=(0, 1))
    filter_rows = [None] * (reach + 1)
    g_ext = jnp.zeros((seqs, local_len + reach, inner), jnp.float32)
    for lag in range(reach + 1):
        masked = g_pre * same[lag]
        filter_rows[reach - lag] = jnp.sum(masked * taps[lag], axis=(0, 1))
        g_ext = g_ext + jnp.pad(filter_weight[reach - lag] * masked, ((0, 0), (reach - lag, lag), (0, 0)))
    filter_grad = jnp.stack(filter_rows)
    returned = from_behind(g_ext[:, :reach], "ctx", -1)
    g_conv_in = g_ext[:, reach:] + jnp.pad(returned, ((0, 0), (local_len - reach, 0), (0, 0)))
    g_conv_in = g_conv_in.reshape(rows, inner).astype(BF16)
    if fast:
        final = finish_weights(x, results[1][1], g_conv_in, results[1][0])
        gate_grads.append(final[0:2])
        conv_grad = jnp.concatenate([final[2:4], final[4:6]], axis=2)
        out_grads.append(final[6])
    else:
        conv_grad = summed(terms_of(x[:modes], lax.all_gather(g_conv_in, "shard", axis=0, tiled=True)))
    in_grad = jnp.stack([conv_grad, jnp.concatenate(gate_grads, axis=2)], axis=2)
    out_grad = jnp.concatenate(out_grads, axis=1).T
    group = lax.axis_size("shard") * lax.axis_size("ctx")
    terms = jnp.concatenate(
        [delta_terms.reshape(modes * group, -1, inner), select_terms.reshape(modes * group, -1, inner)], axis=1
    ).astype(BF16)
    terms = terms.reshape(modes, group, -1, inner).transpose(1, 0, 2, 3).reshape(group, -1, inner)
    terms = jnp.pad(terms, ((0, 0), (0, -terms.shape[1] % 16), (0, 0)))
    terms = lax.psum_scatter(terms, ("shard", "ctx"), scatter_dimension=0, tiled=True)[0].astype(jnp.float32)
    deep = rank // group
    terms = terms[: modes * (terms.shape[0] // modes)]
    each = deep + full_select.shape[1] // group
    terms = terms[: modes * each].reshape(modes, each, inner)
    delta_grad, select_grad = terms[:, :deep], terms[:, deep:]

    g_normed_part = sum(
        product(grad * masks[index], weight[index], 1, 1)
        for weight, grad in ((conv_weight, g_conv_in), (gate_weight, g_gate))
        for index in range(modes)
    )
    row_total = lax.psum(jnp.sum(g_normed_part * norm_gain * whole, axis=1, keepdims=True), "tp")
    gain_part = jnp.sum(g_normed_part * whole * inverse, axis=0)
    scalars = jnp.stack([stream_sq * (1.0 / tps), jnp.sum(mix_local * mix_local), count * (1.0 / tps)])
    small = jnp.concatenate([bias_grad, decay_grad, skip_grad[None], filter_grad, offset_grad[None]], axis=0)
    if fast and width == inner and small.shape[0] == 24:
        wide = jnp.stack([gain_part, jnp.pad(scalars, (0, width - 3))])
        sums = small_sum(jnp.concatenate([small, jnp.pad(wide, ((0, 6), (0, 0)))], axis=0))
        small_total, gain_total, scalars = sums[:24], sums[24], sums[25, :3]
    else:
        small_total = lax.psum(small, ("shard", "ctx"))
        wide = lax.psum(jnp.concatenate([gain_part, scalars]), ("shard", "ctx", "tp"))
        gain_total, scalars = wide[:width], wide[width:]
    g_normed = lax.psum_scatter(
        g_normed_part.astype(BF16), "tp", scatter_dimension=1, tiled=True
    ).astype(jnp.float32)
    start = lax.axis_index("tp") * part_width
    own_gain = lax.dynamic_slice_in_dim(norm_gain, start, part_width, 0)
    g_stream = inverse * own_gain * g_normed - local_stream * inverse**3 * row_total / width
    gain_grad = lax.dynamic_slice_in_dim(gain_total, start, part_width, 0)
    upstream_local = upstream.reshape(rows, part_width).astype(jnp.float32)
    stream_gradient = (upstream_local + g_stream).astype(BF16).reshape(seqs, local_len, part_width)

    denominator = jnp.maximum(scalars[2], 1.0) * width
    stream_rms = jnp.sqrt(scalars[0] / denominator)
    mixer_rms = jnp.sqrt(scalars[1] / denominator)
    return (
        output,
        stream_gradient,
        gain_grad,
        in_grad,
        select_grad,
        delta_grad,
        small_total[:modes],
        out_grad,
        small_total[modes + states + 1 : modes + states + 2 + reach],
        small_total[modes + states + 2 + reach],
        small_total[modes : modes + states],
        small_total[modes + states],
        stream_rms,
        mixer_rms,
    )


def solution(mesh):
    return jax.shard_map(
        per_device,
        mesh=mesh,
        in_specs=(
            P("shard", "ctx", "tp"),
            P(),
            P(None, "shard", None, "tp"),
            P(None, "shard", "tp"),
            P(None, "shard", "tp"),
            P(None, "tp"),
            P("tp", "shard"),
            P(None, "tp"),
            P("tp"),
            P(None, "tp"),
            P("tp"),
            P("shard", None),
            P("shard", "ctx"),
            P("shard", "ctx"),
            P("shard", "ctx", "tp"),
        ),
        out_specs=(
            P("shard", "ctx", "tp"),
            P("shard", "ctx", "tp"),
            P("tp"),
            P(None, ("shard", "ctx"), None, "tp"),
            P(None, ("shard", "ctx"), "tp"),
            P(None, ("shard", "ctx"), "tp"),
            P(None, "tp"),
            P("tp", ("shard", "ctx")),
            P(None, "tp"),
            P("tp"),
            P(None, "tp"),
            P("tp"),
            P(),
            P(),
        ),
        check_vma=False,
    )
```

```python
import functools
import jax
import jax.numpy as jnp
from jax import lax
from jax.experimental import pallas as pl
from jax.experimental.pallas import tpu as pltpu

LOG2E = 1.4426950408889634
VMEM_LIMIT = 60 * 1024 * 1024


def sigmoid(value):
    return 1.0 / (1.0 + jnp.exp(-value))


def softplus(value):
    return jnp.maximum(value, 0.0) + jnp.log1p(jnp.exp(-jnp.abs(value)))


def stage_rows(raw_ref, conv_ref, gate_ref, gg_ref, delta_s, conv_s, g_s, groups):
    def step(block, _):
        top = pl.multiple_of(block * 16, 16)
        for group in range(groups):
            lanes = slice(group * 128, group * 128 + 128)
            delta = softplus(raw_ref[pl.ds(top, 16), lanes])
            conv = conv_ref[pl.ds(top, 16), lanes].astype(jnp.float32)
            gate = gate_ref[pl.ds(top, 16), lanes]
            g_mixed = gg_ref[pl.ds(top, 16), lanes] * (gate * sigmoid(gate))
            for part in range(2):
                rows = pl.ds(pl.multiple_of(((block * 2 + part) * groups + group) * 8, 8), 8)
                eight = slice(part * 8, part * 8 + 8)
                delta_s[rows, :] = delta[eight]
                conv_s[rows, :] = conv[eight]
                g_s[rows, :] = g_mixed[eight]
        return 0

    lax.fori_loop(0, raw_ref.shape[0] // 16, step, 0)


def ends_of(first, tokens, groups, states, a_ref, b_ref, c_ref, cut_ref, delta_s, conv_s, g_s):
    def eight_tokens(tile, carry):
        h, p, l = (list(part) for part in carry)
        for i in range(8):
            rows = pl.ds(tile * (groups * 8) + i, groups, stride=8)
            delta = delta_s[rows, :]
            signal = delta * conv_s[rows, :]
            g = g_s[rows, :]
            token = first + tile * 8 + i
            reach = delta + cut_ref[token]
            for n in range(states):
                decay = jnp.exp2(reach * a_ref[n])
                h[n] = decay * h[n] + signal * b_ref[token * states + n]
                p[n] = decay * p[n]
                l[n] = l[n] + p[n] * (g * c_ref[token * states + n])
        return tuple(h), tuple(p), tuple(l)

    zero = tuple(jnp.zeros((groups, 128), jnp.float32) for _ in range(states))
    one = tuple(jnp.ones((groups, 128), jnp.float32) for _ in range(states))
    return lax.fori_loop(0, tokens // 8, eight_tokens, (zero, one, zero))


def ends_kernel(groups, states, raw_ref, conv_ref, gate_ref, gg_ref, a_ref, b_ref, c_ref,
                cut_ref, h_ref, p_ref, l_ref, delta_s, conv_s, g_s):
    tokens = raw_ref.shape[0]
    stage_rows(raw_ref, conv_ref, gate_ref, gg_ref, delta_s, conv_s, g_s, groups)
    h, p, l = ends_of(pl.program_id(0) * tokens, tokens, groups, states, a_ref, b_ref, c_ref, cut_ref,
                      delta_s, conv_s, g_s)
    for n in range(states):
        h_ref[n], p_ref[n], l_ref[n] = h[n], p[n], l[n]


def entering_kernel(groups, states, seqs, raw_ref, conv_ref, gate_ref, gg_ref, a_ref, b_ref, c_ref, cut_ref,
                    normed_ref, gmix_ref, flag_ref, h0_ref, q0_ref, normed_group, gmix_group, flag_group, delta_s,
                    conv_s, g_s, ahead, behind, before, after, up_send, up_recv, down_send, down_recv, row_send,
                    row_recv, stay_sem):
    shard, ctx = lax.axis_index("shard"), lax.axis_index("ctx")
    block, seq = pl.program_id(0), pl.program_id(1)
    step = block * seqs + seq
    steps = ahead.shape[0]
    tokens = raw_ref.shape[0]
    rows, deep = normed_ref.shape[0], normed_ref.shape[1] // 4

    def remote(source, target, send_sem, recv_sem, to):
        return pltpu.make_async_remote_copy(src_ref=source, dst_ref=target, send_sem=send_sem, recv_sem=recv_sem,
                                            device_id=to, device_id_type=MESH)

    def features(owner):
        return pl.ds(pl.multiple_of(owner * deep, deep), deep)

    def from_me():
        mine = pl.ds(pl.multiple_of(shard * rows, rows), rows)
        return normed_group.at[mine], gmix_group.at[mine], flag_group.at[:, mine]

    def row_copies(k):
        peer = lax.rem(shard + k, 4)
        sources = (normed_ref.at[:, features(peer)], gmix_ref.at[:, features(peer)], flag_ref)
        return [remote(s, t, row_send.at[k - 1, i], row_recv.at[k - 1, i], {"shard": peer})
                for i, (s, t) in enumerate(zip(sources, from_me()))]

    def stays():
        sources = (normed_ref.at[:, features(shard)], gmix_ref.at[:, features(shard)], flag_ref)
        return [pltpu.make_async_copy(s, t, stay_sem.at[i]) for i, (s, t) in enumerate(zip(sources, from_me()))]

    def up(i, d):
        return remote(ahead.at[i], before.at[d - 1, i], up_send.at[i, d - 1], up_recv.at[i, d - 1], {"ctx": ctx + d})

    def down(i, d):
        return remote(behind.at[i], after.at[d - 1, i], down_send.at[i, d - 1], down_recv.at[i, d - 1],
                      {"ctx": ctx - d})

    @pl.when(step == 0)
    def _():
        barrier = pltpu.get_barrier_semaphore()
        for k in range(1, 4):
            pl.semaphore_signal(barrier, inc=1, device_id={"shard": lax.rem(shard + k, 4)}, device_id_type=MESH)
            pl.semaphore_signal(barrier, inc=1, device_id={"ctx": lax.rem(ctx + k, 4)}, device_id_type=MESH)
        pl.semaphore_wait(barrier, 6)
        for k in range(1, 4):
            for copy in row_copies(k):
                copy.start()
        for copy in stays():
            copy.start()
        for d in range(1, 4):
            @pl.when(ctx < d)
            def _():
                before[d - 1] = jnp.zeros(before.shape[1:], before.dtype)

            @pl.when(ctx + d > 3)
            def _():
                after[d - 1] = jnp.zeros(after.shape[1:], after.dtype)

    stage_rows(raw_ref, conv_ref, gate_ref, gg_ref, delta_s, conv_s, g_s, groups)
    h, p, l = ends_of(seq * tokens, tokens, groups, states, a_ref, b_ref, c_ref, cut_ref, delta_s, conv_s, g_s)
    for n in range(0, states, 2):
        for k, values in enumerate((h, p)):
            both = jnp.concatenate([values[n], values[n + 1]], axis=0).astype(ahead.dtype)
            ahead[step, k, n * groups : (n + 2) * groups, :] = both
        for k, values in enumerate((l, p)):
            both = jnp.concatenate([values[n], values[n + 1]], axis=0).astype(behind.dtype)
            behind[step, k, n * groups : (n + 2) * groups, :] = both

    for d in range(1, 4):
        @pl.when(ctx + d < 4)
        def _():
            up(step, d).start()

        @pl.when(ctx >= d)
        def _():
            down(step, d).start()

    @pl.when(step == steps - 1)
    def _():
        for d in range(1, 4):
            for i in range(steps):
                @pl.when(ctx >= d)
                def _():
                    up(i, d).wait_recv()
                    down(i, d).wait_send()

                @pl.when(ctx + d < 4)
                def _():
                    up(i, d).wait_send()
                    down(i, d).wait_recv()

        for i in range(steps):
            for out, got in ((h0_ref, before), (q0_ref, after)):
                total = got[2, i, 0].astype(jnp.float32)
                for d in (1, 0):
                    total = got[d, i, 1].astype(jnp.float32) * total + got[d, i, 0].astype(jnp.float32)
                out[i] = total
        for k in range(1, 4):
            for copy in row_copies(k):
                copy.wait()
        for copy in stays():
            copy.wait()


def scan_kernel(groups, states, fsplit, bsplit, raw_ref, conv_ref, gate_ref, gg_ref, skip_ref, a_ref, h0_ref,
                q0_ref, b_ref, c_ref, cut_ref, gated_ref, ggate_ref, graw_ref, gconv_ref,
                ga_ref, gb_ref, gc_ref, gskip_ref, delta_s, conv_s, g_s, y_s, gs_s, h_s):
    tokens = raw_ref.shape[0]
    tiles = tokens // 8
    first = pl.program_id(0) * tokens
    stage_rows(raw_ref, conv_ref, gate_ref, gg_ref, delta_s, conv_s, g_s, groups)
    lane = lax.broadcasted_iota(jnp.int32, (groups, 128), 1)

    def split_sum(total, names, values, i):
        for n, value in zip(names, values):
            total = jnp.where(lane == i * states + n, jnp.sum(value, axis=1, keepdims=True), total)
        return total

    for low in range(0, states, fsplit):
        names = range(low, low + fsplit)

        def forward(tile, h):
            h = list(h)
            gc = jnp.zeros((groups, 128), jnp.float32) if low == 0 else gc_ref[tile]
            for i in range(8):
                rows = pl.ds(tile * (groups * 8) + i, groups, stride=8)
                delta = delta_s[rows, :]
                signal = delta * conv_s[rows, :]
                g = g_s[rows, :]
                token = tile * 8 + i
                at = (first + token) * states
                reach = delta + cut_ref[first + token]
                y = None
                parts = []
                for k, n in enumerate(names):
                    h_s[token, n] = h[k]
                    decay = jnp.exp2(reach * a_ref[n])
                    h[k] = decay * h[k] + signal * b_ref[at + n]
                    term = h[k] * c_ref[at + n]
                    y = term if y is None else y + term
                    parts.append(h[k] * g)
                gc = split_sum(gc, names, parts, i)
                y_s[rows, :] = y if low == 0 else y + y_s[rows, :]
            gc_ref[tile] = gc
            return tuple(h)

        lax.fori_loop(0, tiles, forward, tuple(h0_ref[n] for n in names))

    def between(block, total):
        top = pl.multiple_of(block * 16, 16)
        new = []
        for group in range(groups):
            lanes = slice(group * 128, group * 128 + 128)
            gate = gate_ref[pl.ds(top, 16), lanes]
            sig = sigmoid(gate)
            y, conv, g = (
                jnp.concatenate([ref[pl.ds(pl.multiple_of(((block * 2 + part) * groups + group) * 8, 8), 8), :]
                                 for part in range(2)], axis=0)
                for ref in (y_s, conv_s, g_s)
            )
            mixed = y + skip_ref[:, lanes] * conv
            gated_ref[pl.ds(top, 16), lanes] = (mixed * (gate * sig)).astype(jnp.bfloat16)
            g_gate = gg_ref[pl.ds(top, 16), lanes] * mixed * sig * (1.0 + gate * (1.0 - sig))
            ggate_ref[pl.ds(top, 16), lanes] = g_gate.astype(jnp.bfloat16)
            product = g * conv
            new.append(total[group] + product[:8] + product[8:])
        return tuple(new)

    sums = lax.fori_loop(0, tokens // 16, between,
                         tuple(jnp.zeros((8, 128), jnp.float32) for _ in range(groups)))
    for group in range(groups):
        gskip_ref[:, group * 128:group * 128 + 128] = sums[group]

    for low in range(0, states, bsplit):
        names = range(low, low + bsplit)

        def backward(step, carry):
            q, ga = (list(part) for part in carry)
            tile = tiles - 1 - step
            gb = jnp.zeros((groups, 128), jnp.float32) if low == 0 else gb_ref[tile]
            for i in reversed(range(8)):
                rows = pl.ds(tile * (groups * 8) + i, groups, stride=8)
                delta = delta_s[rows, :]
                conv = conv_s[rows, :]
                signal = delta * conv
                g = g_s[rows, :]
                token = tile * 8 + i
                at = (first + token) * states
                reach = delta + cut_ref[first + token]
                gd = gs = None
                parts = []
                for k, n in enumerate(names):
                    decay = jnp.exp2(reach * a_ref[n])
                    lam = q[k] + g * c_ref[at + n]
                    q[k] = decay * lam
                    w = q[k] * h_s[token, n]
                    ga[k] = ga[k] + w * delta
                    d_term = w * a_ref[n]
                    s_term = lam * b_ref[at + n]
                    gd = d_term if gd is None else gd + d_term
                    gs = s_term if gs is None else gs + s_term
                    parts.append(lam * signal)
                gb = split_sum(gb, names, parts, i)
                y_s[rows, :] = gd if low == 0 else gd + y_s[rows, :]
                gs_s[rows, :] = gs if low == 0 else gs + gs_s[rows, :]
            gb_ref[tile] = gb
            return tuple(q), tuple(ga)

        zero = tuple(jnp.zeros((groups, 128), jnp.float32) for _ in names)
        _, ga = lax.fori_loop(0, tiles, backward, (tuple(q0_ref[n] for n in names), zero))
        for k, n in enumerate(names):
            ga_ref[n] = ga[k]

    def after(block, _):
        top = pl.multiple_of(block * 16, 16)
        for group in range(groups):
            lanes = slice(group * 128, group * 128 + 128)
            raw = raw_ref[pl.ds(top, 16), lanes]
            gd, gs, conv, delta, g = (
                jnp.concatenate([ref[pl.ds(pl.multiple_of(((block * 2 + part) * groups + group) * 8, 8), 8), :]
                                 for part in range(2)], axis=0)
                for ref in (y_s, gs_s, conv_s, delta_s, g_s)
            )
            g_delta = gd * (1.0 / LOG2E) + conv * gs
            graw_ref[pl.ds(top, 16), lanes] = (g_delta * sigmoid(raw)).astype(jnp.bfloat16)
            gconv_ref[pl.ds(top, 16), lanes] = skip_ref[:, lanes] * g + delta * gs
        return 0

    lax.fori_loop(0, tokens // 16, after, 0)


def sizes(raw, seqs, states):
    rows, inner = raw.shape
    groups = min(8, inner // 128)
    return rows // seqs, inner // (groups * 128), groups


def state_form(value, blocks, groups):
    states = value.shape[0]
    return value.reshape(states, blocks, groups, 128).transpose(1, 0, 2, 3)


def from_state_form(value):
    blocks, states, groups, lanes = value.shape
    return value.transpose(1, 0, 2, 3).reshape(states, blocks * groups * lanes)


def token_spec(tokens, width, block):
    return pl.BlockSpec((tokens, width), lambda s: (s, block))


def state_spec(states, groups):
    return pl.BlockSpec((None, states, groups, 128), lambda s: (s, 0, 0, 0))


def scan_ends(raw, conv, gate, gg, a2, b, c, cut, seqs, block):
    states, groups, _ = a2.shape
    tokens = raw.shape[0] // seqs
    width = groups * 128
    smem = pl.BlockSpec(memory_space=pltpu.SMEM)
    out = jax.ShapeDtypeStruct((seqs, states, groups, 128), jnp.float32)
    elements = raw.shape[0] * width * states
    return pl.pallas_call(
        functools.partial(ends_kernel, groups, states),
        grid=(seqs,),
        in_specs=[token_spec(tokens, width, block)] * 4
        + [pl.BlockSpec((states, groups, 128), lambda s: (0, 0, 0)), smem, smem, smem],
        out_specs=[state_spec(states, groups)] * 3,
        out_shape=[out] * 3,
        scratch_shapes=[pltpu.VMEM((tokens * groups, 128), jnp.float32)] * 3,
        compiler_params=pltpu.CompilerParams(vmem_limit_bytes=VMEM_LIMIT),
        cost_estimate=pl.CostEstimate(flops=8 * elements, bytes_accessed=elements, transcendentals=elements),
        name="scan_ends",
    )(raw, conv, gate, gg, a2, b.reshape(-1), c.reshape(-1), cut.reshape(-1))


def scan_both(raw, conv, gate, gg, skip, a2, h0, q0, b, c, cut, seqs, block):
    states, groups, _ = a2.shape
    rows, inner = raw.shape
    tokens = rows // seqs
    width = groups * 128
    smem = pl.BlockSpec(memory_space=pltpu.SMEM)
    elements = rows * width * states
    token = token_spec(tokens, width, block)
    tiles = tokens // 8
    own = pl.BlockSpec((tokens, width), lambda s: (s, 0))
    pair = pl.BlockSpec((tiles, groups, 128), lambda s: (s, 0, 0))
    pair_shape = jax.ShapeDtypeStruct((rows // 8, groups, 128), jnp.float32)
    low = jax.ShapeDtypeStruct((rows, width), jnp.bfloat16)
    return pl.pallas_call(
        functools.partial(scan_kernel, groups, states, states, states),
        grid=(seqs,),
        in_specs=[token] * 4
        + [pl.BlockSpec((1, width), lambda s: (0, block)),
           pl.BlockSpec((states, groups, 128), lambda s: (0, 0, 0)),
           state_spec(states, groups), state_spec(states, groups), smem, smem, smem],
        out_specs=[own] * 4 + [state_spec(states, groups), pair, pair,
                               pl.BlockSpec((None, 8, width), lambda s: (s, 0, 0))],
        out_shape=[low, low, low, jax.ShapeDtypeStruct((rows, width), jnp.float32),
                   jax.ShapeDtypeStruct((seqs, states, groups, 128), jnp.float32),
                   pair_shape, pair_shape, jax.ShapeDtypeStruct((seqs, 8, width), jnp.float32)],
        scratch_shapes=[pltpu.VMEM((tokens * groups, 128), jnp.float32)] * 5
        + [pltpu.VMEM((tokens, states, groups, 128), jnp.float32)],
        compiler_params=pltpu.CompilerParams(vmem_limit_bytes=VMEM_LIMIT),
        cost_estimate=pl.CostEstimate(flops=22 * elements, bytes_accessed=2 * elements, transcendentals=2 * elements),
        name="scan_both",
    )(raw, conv, gate, gg, skip.reshape(1, inner), a2, h0, q0, b.reshape(-1), c.reshape(-1), cut.reshape(-1))


def pair_sum(value, states):
    return jnp.sum(value, axis=1).reshape(-1, states)


MESH = pl.DeviceIdType.MESH


def gather_kernel(chunks, conv_ref, gate_ref, out_ref, conv_full, gate_full, out_full, local_sem, core_send,
                  core_recv, y_send, y_recv, z_send, z_recv, pass_send, pass_recv, rest_send, rest_recv):
    shard, ctx = lax.axis_index("shard"), lax.axis_index("ctx")
    mine, far = shard, lax.rem(shard + 2, 4)
    core = {"shard": shard + 1 - 2 * lax.rem(shard, 2)}
    across = {"shard": far}
    side = {"ctx": ctx + 1 - 2 * lax.rem(ctx, 2)}
    half = lax.rem(ctx, 2)
    depth = conv_ref.shape[1]
    columns = out_ref.shape[1]
    piece = depth // 2 // chunks
    piece_out = out_ref.shape[0] // 2 // chunks

    barrier = pltpu.get_barrier_semaphore()
    for peer in (core, across, side):
        pl.semaphore_signal(barrier, inc=1, device_id=peer, device_id_type=MESH)
    pl.semaphore_wait(barrier, 3)

    def views(owner, part, i):
        rows = pl.ds(pl.multiple_of(owner * depth + (part * chunks + i) * piece, piece), piece)
        tall = pl.ds(pl.multiple_of((part * chunks + i) * piece_out, piece_out), piece_out)
        wide = pl.ds(pl.multiple_of(owner * columns, columns), columns)
        return conv_full.at[:, rows], gate_full.at[:, rows], out_full.at[tall, wide]

    def own(part, i):
        rows = pl.ds(pl.multiple_of((part * chunks + i) * piece, piece), piece)
        tall = pl.ds(pl.multiple_of((part * chunks + i) * piece_out, piece_out), piece_out)
        return conv_ref.at[:, rows], gate_ref.at[:, rows], out_ref.at[tall, :]

    def send(source, target, to, send_sem, recv_sem):
        copies = [
            pltpu.make_async_remote_copy(src_ref=s, dst_ref=t, send_sem=send_sem.at[k], recv_sem=recv_sem.at[k],
                                         device_id=to, device_id_type=MESH)
            for k, (s, t) in enumerate(zip(source, target))
        ]
        for copy in copies:
            copy.start()
        return copies

    def cross(i):
        return send(own(half, i), views(mine, half, i), across, y_send.at[i], y_recv.at[i])

    to_far = [cross(i) for i in range(min(2, chunks))]
    rows = pl.ds(pl.multiple_of(mine * depth, depth), depth)
    wide = pl.ds(pl.multiple_of(mine * columns, columns), columns)
    source = (conv_ref, gate_ref, out_ref)
    place = (conv_full.at[:, rows], gate_full.at[:, rows], out_full.at[:, wide])
    stay = [pltpu.make_async_copy(s, t, local_sem.at[k]) for k, (s, t) in enumerate(zip(source, place))]
    for copy in stay:
        copy.start()
    to_core = send(source, place, core, core_send, core_recv)
    onward = []
    for i in range(chunks):
        for copy in to_far[i]:
            copy.wait()
        if i + 2 < chunks:
            to_far.append(cross(i + 2))
        held = views(far, half, i)
        onward.append(send(held, held, side, z_send.at[i], z_recv.at[i]))
        to_core += send(held, held, core, pass_send.at[i], pass_recv.at[i])
    for i in range(chunks):
        for copy in onward[i]:
            copy.wait_recv()
        held = views(far, 1 - half, i)
        to_core += send(held, held, core, rest_send.at[i], rest_recv.at[i])
    for copy in stay:
        copy.wait()
    for copy in to_core:
        copy.wait()
    for i in range(chunks):
        for copy in onward[i]:
            copy.wait_send()


def gather_weights(in_own, out_own, chunks=8):
    _, modes, depth, inner = in_own.shape
    any_space = pl.BlockSpec(memory_space=pl.ANY)
    vmem = pl.BlockSpec(memory_space=pltpu.VMEM)
    many = pltpu.SemaphoreType.DMA((chunks, 3))
    three = pltpu.SemaphoreType.DMA((3,))
    full = jax.ShapeDtypeStruct((modes, 4 * depth, inner), in_own.dtype)
    return pl.pallas_call(
        functools.partial(gather_kernel, chunks),
        in_specs=[vmem] * 3,
        out_specs=[any_space] * 3,
        out_shape=[full, full, jax.ShapeDtypeStruct((inner, 4 * out_own.shape[1]), out_own.dtype)],
        scratch_shapes=[three] * 3 + [many] * 8,
        compiler_params=pltpu.CompilerParams(collective_id=1, has_side_effects=True, vmem_limit_bytes=32 * 2**20),
        cost_estimate=pl.CostEstimate(flops=0, bytes_accessed=400_000_000, transcendentals=0),
        name="gather_weights",
    )(in_own[0], in_own[1], out_own)


def finish_kernel(x_ref, first_0, first_1, first_2, first_3, conv_ref, gated_ref, gate_ref, mask_ref, conv_weight,
                  gate_weight, sum_ref, normed_ref, other_ref, blocks, part, came, gate_s, weight_s, give_s, y_send,
                  y_recv, core_send, core_recv, pass_send, pass_recv, local_sem, first_sem, gate_sem, weight_sem,
                  x_sem, up_send, up_recv, down_send, down_recv):
    shard, ctx, tp = lax.axis_index("shard"), lax.axis_index("ctx"), lax.axis_index("tp")
    far = lax.rem(shard + 2, 4)
    core = {"shard": shard + 1 - 2 * lax.rem(shard, 2)}
    across = {"shard": far}
    jobs, units, last = blocks.shape[0], part.shape[0], 3
    tokens, width = gated_ref.shape
    deep, narrow = sum_ref.shape[1:]
    up, down, beside = {"ctx": ctx + 1}, {"ctx": ctx - 1}, {"tp": 1 - tp}
    features = weight_s.shape[3]
    steps = normed_ref.shape[1] // features

    barrier = pltpu.get_barrier_semaphore()
    for peer in (core, across, beside):
        pl.semaphore_signal(barrier, inc=1, device_id=peer, device_id_type=MESH)

    @pl.when(ctx < last)
    def _():
        pl.semaphore_signal(barrier, inc=1, device_id=up, device_id_type=MESH)

    @pl.when(ctx > 0)
    def _():
        pl.semaphore_signal(barrier, inc=1, device_id=down, device_id_type=MESH)

    pl.semaphore_wait(barrier, 3 + jnp.where(ctx < last, 1, 0) + jnp.where(ctx > 0, 1, 0))

    sources = [None, conv_ref.at[:, pl.ds(0, width)], conv_ref.at[:, pl.ds(width, width)], gated_ref]

    def rows_of(owner):
        return pl.ds(pl.multiple_of(owner * tokens, tokens), tokens)

    def remote(source, target, send_sem, recv_sem, to):
        return pltpu.make_async_remote_copy(src_ref=source, dst_ref=target, send_sem=send_sem, recv_sem=recv_sem,
                                            device_id=to, device_id_type=MESH)

    def cross(j):
        return remote(sources[j], blocks.at[j, rows_of(shard)], y_send.at[j], y_recv.at[j], across)

    def pair(j):
        return remote(sources[j], blocks.at[j, rows_of(shard)], core_send.at[j], core_recv.at[j], core)

    def onward(j):
        held = blocks.at[j, rows_of(far)]
        return remote(held, held, pass_send.at[j], pass_recv.at[j], core)

    def stay(j):
        return pltpu.make_async_copy(sources[j], blocks.at[j, rows_of(shard)], local_sem.at[j])

    def advance(j):
        cross(j).wait()
        onward(j).start()
        if j + 2 < jobs:
            cross(j + 2).start()

    def hop(u, k, slot, send_sem, recv_sem, to):
        rows = pl.ds(pl.multiple_of(k * deep, deep), deep)
        there = pl.ds(pl.multiple_of(slot * deep, deep), deep)
        return remote(part.at[u, rows], came.at[u, there], send_sem.at[u, k], recv_sem.at[u, k], to)

    def going_up(u, k):
        return hop(u, k, k, up_send, up_recv, up)

    def going_down(u, k):
        return hop(u, k, jnp.where(k == ctx - 1, last + 1, k), down_send, down_recv, down)

    def coming_down(u, k):
        return hop(u, k, jnp.where(k == ctx, last + 1, k), down_send, down_recv, down)

    def add(u, k):
        rows = pl.ds(k * deep, deep)
        total = part[u, rows, :].astype(jnp.float32) + came[u, rows, :].astype(jnp.float32)
        part[u, rows, :] = total.astype(part.dtype)

    def feature_rows(i):
        return pl.multiple_of(lax.rem(i + (1 - tp) * (steps // 2), steps) * features, features)

    def load(i, slot):
        rows = pl.ds(feature_rows(i), features)
        return [pltpu.make_async_copy(ref.at[:, rows], weight_s.at[slot, k], weight_sem.at[slot, k])
                for k, ref in enumerate((conv_weight, gate_weight))]

    def beside_copy():
        return remote(give_s, other_ref, x_sem.at[0], x_sem.at[1], beside)

    owners = (shard, shard + 1 - 2 * lax.rem(shard, 2), far, 3 - shard)
    firsts = [pltpu.make_async_copy(ref, blocks.at[0, rows_of(owner)], first_sem.at[k])
              for k, (owner, ref) in enumerate(zip(owners, (first_0, first_1, first_2, first_3)))]
    for copy in firsts:
        copy.start()
    for j in range(1, min(3, jobs)):
        cross(j).start()
    own_gate = pltpu.make_async_copy(gate_ref, gate_s, gate_sem.at[0])
    own_gate.start()
    for j in range(1, jobs):
        stay(j).start()
        pair(j).start()
    for copy in load(0, 0):
        copy.start()
    for copy in firsts:
        copy.wait()
    own_gate.wait()
    for j in range(1, jobs):
        stay(j).wait()

    def step(t, _):
        for j in range(1, jobs):
            @pl.when(t == 4 * j)
            def _():
                pair(j).wait()
                onward(j).wait()

        @pl.when(t < units)
        def _():
            job = t // 4
            which = jnp.where(t >= 4 * (jobs - 1), 2, lax.rem(t // 2, 2))
            column = lax.rem(t, 2) * narrow
            for c in range(narrow // 256):
                lanes = pl.ds(pl.multiple_of(column + c * 256, 256), 256)
                part[t, :, c * 256 : c * 256 + 256] = jnp.dot(
                    x_ref[which], blocks[job, :, lanes], preferred_element_type=jnp.float32
                ).astype(part.dtype)

        u = t - ctx

        @pl.when((u >= 0) & (u < units))
        def _():
            for k in range(last, 0, -1):
                @pl.when(k > ctx)
                def _():
                    @pl.when(ctx > 0)
                    def _():
                        going_up(u, k).wait_recv()
                        add(u, k)

                    going_up(u, k).start()

        v = t - (last - ctx)

        @pl.when((v >= 0) & (v < units))
        def _():
            for k in range(last):
                @pl.when(k < ctx)
                def _():
                    @pl.when(ctx < last)
                    def _():
                        coming_down(v, k).wait_recv()
                        add(v, k)

                    going_down(v, k).start()

        @pl.when(t < steps)
        def _():
            slot = lax.rem(t, 2)

            @pl.when(t + 1 < steps)
            def _():
                for copy in load(t + 1, 1 - slot):
                    copy.start()

            for copy in load(t, slot):
                copy.wait()
            mine = rows_of(shard)
            left = (blocks[1, mine, :], blocks[2, mine, :], gate_s[...], blocks[0, mine, :])
            total = None
            for k, rows in enumerate(left):
                weight = weight_s[slot, k // 2, :, :, (k % 2) * width : (k % 2) * width + width]
                term = lax.dot_general(rows, weight.reshape(2 * features, width), (((1,), (1,)), ((), ())),
                                       preferred_element_type=jnp.float32)
                total = term if total is None else total + term
            total = mask_ref[:, 0:1] * total[:, :features] + mask_ref[:, 1:2] * total[:, features:]
            at = feature_rows(t)
            normed_ref[:, pl.ds(at, features)] = total

            @pl.when(t < steps // 2)
            def _():
                give_s[:, pl.ds(pl.multiple_of(t * features, features), features)] = total.astype(give_s.dtype)

            @pl.when(t == steps // 2)
            def _():
                beside_copy().start()

        w = t - last

        @pl.when(w >= 0)
        def _():
            rows = pl.ds(pl.multiple_of(ctx * deep, deep), deep)
            sum_ref[w] = part[w, rows, :].astype(jnp.float32)

            @pl.when(ctx > 0)
            def _():
                going_up(w, ctx).wait_recv()
                sum_ref[w] += came[w, rows, :].astype(jnp.float32)

            @pl.when(ctx < last)
            def _():
                coming_down(w, ctx).wait_recv()
                sum_ref[w] += came[w, (last + 1) * deep :, :].astype(jnp.float32)

        for j in range(1, jobs):
            @pl.when(t == 4 * j - 2)
            def _():
                advance(j)

        return 0

    lax.fori_loop(0, units + last, step, 0)
    beside_copy().wait()

    def drain(u, _):
        for k in range(last + 1):
            @pl.when(k > ctx)
            def _():
                going_up(u, k).wait_send()

            @pl.when(k < ctx)
            def _():
                going_down(u, k).wait_send()

        return 0

    lax.fori_loop(0, units, drain, 0)


def finish_weights(x, first, g_conv_in, gated, g_gate, masks, conv_weight, gate_weight):
    _, features, group = x.shape
    tokens, width = gated.shape
    jobs, units, narrow = 4, 14, width // 2
    deep = features // 4
    total = conv_weight.shape[1]
    any_space = pl.BlockSpec(memory_space=pl.ANY)
    vmem = pl.BlockSpec(memory_space=pltpu.VMEM)
    sums = pltpu.SemaphoreType.DMA((units, 4))
    job_sems = pltpu.SemaphoreType.DMA((jobs,))
    two = pltpu.SemaphoreType.DMA((2,))
    flops = 2 * units * features * group * narrow + 8 * tokens * total * 2 * width * 2
    return pl.pallas_call(
        finish_kernel,
        in_specs=[vmem] + [any_space] * 7 + [vmem] + [any_space] * 2,
        out_specs=[vmem] * 3,
        out_shape=[jax.ShapeDtypeStruct((units, deep, narrow), jnp.float32),
                   jax.ShapeDtypeStruct((tokens, total), jnp.float32),
                   jax.ShapeDtypeStruct((tokens, total // 2), jnp.bfloat16)],
        scratch_shapes=[pltpu.VMEM((jobs, group, width), jnp.bfloat16),
                        pltpu.VMEM((units, features, narrow), jnp.bfloat16),
                        pltpu.VMEM((units, 5 * deep, narrow), jnp.bfloat16),
                        pltpu.VMEM((tokens, width), jnp.bfloat16),
                        pltpu.VMEM((2, 2, 2, 128, 2 * width), jnp.bfloat16),
                        pltpu.VMEM((tokens, total // 2), jnp.bfloat16)]
        + [job_sems] * 8 + [two, pltpu.SemaphoreType.DMA((2, 2)), two] + [sums] * 4,
        compiler_params=pltpu.CompilerParams(collective_id=2, has_side_effects=True, vmem_limit_bytes=VMEM_LIMIT),
        cost_estimate=pl.CostEstimate(flops=flops, bytes_accessed=500_000_000, transcendentals=0),
        name="finish_weights",
    )(x, *first, g_conv_in, gated, g_gate, masks, conv_weight, gate_weight)


def scan_entering(raw, conv, gate, gg, a2, b, c, cut, normed, g_mix, flags, seqs):
    blocks, states, groups, _ = a2.shape
    rows = raw.shape[0]
    tokens = rows // seqs
    width = groups * 128
    steps = blocks * seqs
    smem = pl.BlockSpec(memory_space=pltpu.SMEM)
    any_space = pl.BlockSpec(memory_space=pl.ANY)
    vmem = pl.BlockSpec(memory_space=pltpu.VMEM)
    token = pl.BlockSpec((tokens, width), lambda j, s: (s, j))
    elements = raw.size * states
    ends = pltpu.VMEM((steps, 2, states * groups, 128), jnp.bfloat16)
    came = pltpu.VMEM((3, steps, 2, states * groups, 128), jnp.bfloat16)
    sums = pltpu.SemaphoreType.DMA((steps, 3))
    nine = pltpu.SemaphoreType.DMA((3, 3))
    state = jax.ShapeDtypeStruct((steps, states * groups, 128), jnp.float32)
    group = jax.ShapeDtypeStruct((4 * rows, normed.shape[1] // 4), jnp.bfloat16)
    h0, q0, *lists = pl.pallas_call(
        functools.partial(entering_kernel, groups, states, seqs),
        grid=(blocks, seqs),
        in_specs=[token] * 4
        + [pl.BlockSpec((None, states, groups, 128), lambda j, s: (j, 0, 0, 0)), smem, smem, smem]
        + [any_space] * 3,
        out_specs=[vmem] * 2 + [any_space] * 3,
        out_shape=[state, state, group, group, jax.ShapeDtypeStruct((flags.shape[0], 4 * rows), jnp.bfloat16)],
        scratch_shapes=[pltpu.VMEM((tokens * groups, 128), jnp.float32)] * 3 + [ends] * 2 + [came] * 2
        + [sums] * 4 + [nine] * 2 + [pltpu.SemaphoreType.DMA((3,))],
        compiler_params=pltpu.CompilerParams(collective_id=4, has_side_effects=True, vmem_limit_bytes=VMEM_LIMIT),
        cost_estimate=pl.CostEstimate(flops=8 * elements, bytes_accessed=elements, transcendentals=elements),
        name="scan_entering",
    )(raw, conv, gate, gg, a2, b.reshape(-1), c.reshape(-1), cut.reshape(-1), normed, g_mix, flags)
    shape = (blocks, seqs, states, groups, 128)
    return h0.reshape(shape), q0.reshape(shape), lists


def small_kernel(in_ref, out_ref, x_in, mine, y_in, z_in, x_sem, a_send, a_recv, b_send, b_recv, c_send, c_recv):
    shard, ctx, tp = lax.axis_index("shard"), lax.axis_index("ctx"), lax.axis_index("tp")
    quarter = out_ref.shape[0] // 4
    other = {"tp": 1 - tp}

    def shard_peer(k):
        return {"shard": lax.rem(shard + k, 4)}

    def ctx_peer(k):
        return {"ctx": lax.rem(ctx + k, 4)}

    barrier = pltpu.get_barrier_semaphore()
    pl.semaphore_signal(barrier, inc=1, device_id=other, device_id_type=MESH)
    for k in range(1, 4):
        pl.semaphore_signal(barrier, inc=1, device_id=shard_peer(k), device_id_type=MESH)
        pl.semaphore_signal(barrier, inc=1, device_id=ctx_peer(k), device_id_type=MESH)
    pl.semaphore_wait(barrier, 7)

    def remote(source, target, send_sem, recv_sem, to):
        copy = pltpu.make_async_remote_copy(src_ref=source, dst_ref=target, send_sem=send_sem, recv_sem=recv_sem,
                                            device_id=to, device_id_type=MESH)
        copy.start()
        return copy

    def rows_of(k):
        return pl.ds(pl.multiple_of(k * quarter, 8), quarter)

    total = in_ref.shape[0]
    copy = remote(in_ref.at[pl.ds(total - 8, 8)], x_in, x_sem.at[0], x_sem.at[1], other)
    mine[...] = in_ref[...]
    copy.wait()
    mine[total - 8 :, :] = in_ref[total - 8 :, :] + x_in[...]

    copies = [remote(mine.at[rows_of(lax.rem(shard + k, 4))], y_in.at[k - 1], a_send.at[k - 1], a_recv.at[k - 1],
                     shard_peer(k)) for k in range(1, 4)]
    for copy in copies:
        copy.wait()
    z_in[ctx] = mine[rows_of(shard), :] + y_in[0] + y_in[1] + y_in[2]
    copies = [remote(z_in.at[ctx], z_in.at[ctx], b_send.at[k - 1], b_recv.at[k - 1], ctx_peer(k))
              for k in range(1, 4)]
    for copy in copies:
        copy.wait()
    out_ref[rows_of(shard), :] = (z_in[0] + z_in[1]) + (z_in[2] + z_in[3])
    copies = [remote(out_ref.at[rows_of(shard)], out_ref.at[rows_of(shard)], c_send.at[k - 1], c_recv.at[k - 1],
                     shard_peer(k)) for k in range(1, 4)]
    for copy in copies:
        copy.wait()


def small_sum(value):
    rows, width = value.shape
    quarter = rows // 4
    vmem = pl.BlockSpec(memory_space=pltpu.VMEM)
    three = pltpu.SemaphoreType.DMA((3,))
    return pl.pallas_call(
        small_kernel,
        in_specs=[vmem],
        out_specs=vmem,
        out_shape=jax.ShapeDtypeStruct(value.shape, value.dtype),
        scratch_shapes=[pltpu.VMEM((8, width), value.dtype), pltpu.VMEM(value.shape, value.dtype),
                        pltpu.VMEM((3, quarter, width), value.dtype), pltpu.VMEM((4, quarter, width), value.dtype),
                        pltpu.SemaphoreType.DMA((2,))] + [three] * 6,
        compiler_params=pltpu.CompilerParams(collective_id=3, has_side_effects=True, vmem_limit_bytes=32 * 2**20),
        cost_estimate=pl.CostEstimate(flops=0, bytes_accessed=40_000_000, transcendentals=0),
        name="small_sum",
    )(value)


from jax.sharding import PartitionSpec as P

EPSILON = 1e-05
BF16 = jnp.bfloat16


def from_behind(value, axis, by):
    devices = lax.axis_size(axis)
    pairs = [(i, i + by) for i in range(devices) if 0 <= i + by < devices]
    return lax.ppermute(value, axis, pairs)


def product(left, right, left_dim, right_dim):
    return lax.dot_general(
        left, right, (((left_dim,), (right_dim,)), ((), ())), preferred_element_type=jnp.float32
    )


def exchange_ends(last, total, back, axis):
    devices = lax.axis_size(axis)
    state, adjoint = jnp.zeros_like(last), jnp.zeros_like(last)
    ahead = jnp.stack([last, total]).astype(BF16)
    behind = jnp.stack([back, total]).astype(BF16)
    before = [from_behind(ahead, axis, k) for k in range(1, devices)]
    after = [from_behind(behind, axis, -k) for k in range(1, devices)]
    for part in reversed(before):
        state = part[1].astype(jnp.float32) * state + part[0].astype(jnp.float32)
    for part in reversed(after):
        adjoint = part[1].astype(jnp.float32) * adjoint + part[0].astype(jnp.float32)
    return state, adjoint


def group_rows(normed, g_mix, masks):
    both = lax.all_to_all(jnp.stack([normed, g_mix]), "shard", 2, 1, tiled=True)
    flags = lax.all_gather(masks, "shard", axis=1, tiled=True)
    return jnp.stack([(both[0] * flag[:, None]).T for flag in flags] + [both[1].T])


def per_device(
    stream,
    norm_gain,
    in_weight,
    select_weight,
    delta_weight,
    delta_bias,
    out_weight,
    filter_weight,
    filter_bias,
    decay_log,
    skip_gain,
    segments,
    modality,
    valid,
    upstream,
):
    seqs, local_len, part_width = stream.shape
    width = norm_gain.shape[0]
    inner = out_weight.shape[0]
    states = decay_log.shape[0]
    reach = filter_weight.shape[0] - 1
    rows = seqs * local_len
    tps = lax.axis_size("tp")
    modes, depth = in_weight.shape[:2]
    in_own = in_weight.transpose(2, 0, 1, 3)
    fast = (lax.axis_size("shard"), lax.axis_size("ctx"), lax.axis_size("tp")) == (4, 4, 2)
    if fast:
        conv_weight, gate_weight, full_out = gather_weights(in_own, out_weight)
    else:
        conv_weight, gate_weight = lax.all_gather(in_own, "shard", axis=2, tiled=True)
        full_out = lax.all_gather(out_weight, "shard", axis=1, tiled=True)
    full_select = lax.all_gather(select_weight, "shard", axis=1, tiled=True)
    full_delta = lax.all_gather(delta_weight, "shard", axis=1, tiled=True)
    rank = full_delta.shape[1]
    mode_rows = modality.reshape(rows)
    masks = jnp.stack([(mode_rows == index).astype(BF16)[:, None] for index in range(modes)])
    masks_float = masks.astype(jnp.float32)
    valid_rows = valid.reshape(rows, 1).astype(jnp.float32)

    def apply_modes(values, weights, weight_dim):
        total = product(values * masks[0], weights[0], 1, weight_dim)
        for index in range(1, modes):
            total = total + product(values * masks[index], weights[index], 1, weight_dim)
        return total

    def pair_total(value):
        if tps != 2:
            return lax.psum(value, "tp")
        return value + lax.ppermute(value, "tp", [(0, 1), (1, 0)])

    def half_total(sent, value):
        if tps != 2:
            return lax.psum_scatter(sent, "tp", scatter_dimension=1, tiled=True).astype(jnp.float32)
        own = lax.axis_index("tp") * part_width
        gift = lax.dynamic_slice_in_dim(sent, part_width - own, part_width, 1)
        gift = lax.ppermute(gift, "tp", [(0, 1), (1, 0)])
        return lax.dynamic_slice_in_dim(value, own, part_width, 1) + gift.astype(jnp.float32)

    def modal_terms(values, grads):
        return jnp.stack([product(values * masks[index], grads, 0, 0) for index in range(modes)])

    g_mix = lax.all_gather(upstream, "tp", axis=2, tiled=True).reshape(rows, width) * valid_rows.astype(BF16)
    g_gated = product(g_mix, full_out, 1, 1)

    whole = lax.all_gather(stream, "tp", axis=2, tiled=True).reshape(rows, width).astype(jnp.float32)
    inverse = lax.rsqrt(jnp.mean(whole * whole, axis=1, keepdims=True) + EPSILON)
    normed = (whole * inverse * norm_gain).astype(BF16)
    normed_modes = jnp.concatenate([normed * masks[index] for index in range(modes)], axis=1)
    conv_in = product(normed_modes, conv_weight.reshape(modes * width, inner), 1, 0)
    conv_in = conv_in.astype(BF16).reshape(seqs, local_len, inner)
    gate_in = product(normed_modes, gate_weight.reshape(modes * width, inner), 1, 0)

    def terms_of(lefts, grads):
        return jnp.stack([product(left, grads, 1, 0) for left in lefts]).astype(BF16)

    def summed(terms):
        return lax.psum_scatter(terms, "ctx", scatter_dimension=1, tiled=True).astype(jnp.float32)

    edge = from_behind(conv_in[:, local_len - reach :], "ctx", 1)
    extended = jnp.concatenate([edge, conv_in], axis=1).astype(jnp.float32)
    offset = lax.axis_index("ctx") * local_len
    padded = jnp.concatenate([jnp.full((seqs, reach), -1, jnp.int32), segments], axis=1)
    seg_ext = lax.dynamic_slice_in_dim(padded, offset, local_len + reach, 1)
    own_seg = seg_ext[:, reach:]
    same = [
        (seg_ext[:, reach - lag : reach - lag + local_len] == own_seg).astype(jnp.float32)[:, :, None]
        for lag in range(reach + 1)
    ]
    taps = [extended[:, reach - lag : reach - lag + local_len] for lag in range(reach + 1)]
    pre = jnp.zeros((seqs, local_len, inner), jnp.float32) + filter_bias
    for lag in range(reach + 1):
        pre = pre + filter_weight[reach - lag] * taps[lag] * same[lag]
    cut = (1.0 - same[1][:, :, 0]) * 1e30
    conv_out = jax.nn.silu(pre).astype(BF16).reshape(rows, inner)
    selected = pair_total(apply_modes(conv_out, full_select, 1))
    delta_low = selected[:, :rank].astype(BF16)
    b_in = selected[:, rank : rank + states]
    c_out = selected[:, rank + states :]
    bias_rows = sum(masks_float[index] * delta_bias[index] for index in range(modes))
    raw = apply_modes(delta_low, full_delta, 0) + bias_rows

    neg_decay = -jnp.exp(decay_log)
    _, blocks, groups = sizes(raw, seqs, states)
    a2 = state_form(neg_decay * LOG2E, blocks, groups)
    if fast:
        flags = jnp.pad(masks[:, :, 0], ((0, 16 - modes), (0, 0)))
        carried, adjoint, (normed_group, g_mix_group, flags) = scan_entering(
            raw, conv_out, gate_in, g_gated, a2, b_in, c_out, cut, normed, g_mix, flags, seqs
        )
        entering = list(zip(carried, adjoint))
        normed_turned = normed_group.T
        x = jnp.stack([normed_turned * flags[index : index + 1] for index in range(modes)] + [g_mix_group.T])
    else:
        entering = [
            exchange_ends(*scan_ends(raw, conv_out, gate_in, g_gated, a2[j], b_in, c_out, cut, seqs, j), "ctx")
            for j in range(blocks)
        ]
        x = group_rows(normed, g_mix, masks[:, :, 0])
    results = [
        scan_both(raw, conv_out, gate_in, g_gated, skip_gain, a2[j], *entering[j], b_in, c_out, cut, seqs, j)
        for j in range(blocks)
    ]
    early = []
    for part in results[: 1 if fast else blocks]:
        gate_all = lax.all_gather(part[1], "shard", axis=0, tiled=True)
        gated_all = lax.all_gather(part[0], "shard", axis=0, tiled=True)
        early.append((terms_of(x[:modes], gate_all), terms_of(x[modes:], gated_all)))
    if fast:
        first = [results[1][1]] + [
            lax.ppermute(results[1][1], "shard", [(i, i ^ k) for i in range(4)]) for k in range(1, 4)
        ]
    early, results = lax.optimization_barrier((early, results))
    gate_grads = [summed(part[0]) for part in early]
    out_grads = [summed(part[1])[0] for part in early]
    gated, g_gate, g_raw, g_conv, g_neg, g_b, g_c, g_skip = zip(*results)
    gated, g_gate, g_raw, g_conv = (jnp.concatenate(part, axis=1) for part in (gated, g_gate, g_raw, g_conv))
    g_skip = jnp.concatenate(g_skip, axis=2)
    g_neg = jnp.stack([jnp.sum(part, axis=0) for part in g_neg])

    mix_part = product(gated, full_out, 1, 0)
    mix_local = half_total(mix_part.astype(BF16), mix_part) * valid_rows
    local_stream = stream.reshape(rows, part_width).astype(jnp.float32)
    output = (local_stream + mix_local).astype(BF16).reshape(seqs, local_len, part_width)
    stream_sq = jnp.sum(valid_rows * jnp.sum(whole * whole, axis=1, keepdims=True))
    count = jnp.sum(valid_rows)
    skip_grad = jnp.sum(g_skip, axis=(0, 1))
    decay_grad = from_state_form(g_neg) * neg_decay
    bias_grad = product(masks[:, :, 0], g_raw, 1, 0)
    delta_terms = modal_terms(delta_low, g_raw)
    g_low = apply_modes(g_raw, full_delta, 1)
    select_part = jnp.concatenate([g_low, pair_sum(sum(g_b), states), pair_sum(sum(g_c), states)], axis=1)
    g_sel_low = pair_total(select_part).astype(BF16)
    select_terms = modal_terms(g_sel_low, conv_out)
    g_conv = g_conv + apply_modes(g_sel_low, full_select, 0)
    sig_pre = jax.nn.sigmoid(pre)
    g_pre = g_conv.reshape(seqs, local_len, inner) * sig_pre * (1.0 + pre * (1.0 - sig_pre))
    offset_grad = jnp.sum(g_pre, axis=(0, 1))
    filter_rows = [None] * (reach + 1)
    g_ext = jnp.zeros((seqs, local_len + reach, inner), jnp.float32)
    for lag in range(reach + 1):
        masked = g_pre * same[lag]
        filter_rows[reach - lag] = jnp.sum(masked * taps[lag], axis=(0, 1))
        g_ext = g_ext + jnp.pad(filter_weight[reach - lag] * masked, ((0, 0), (reach - lag, lag), (0, 0)))
    filter_grad = jnp.stack(filter_rows)
    returned = from_behind(g_ext[:, :reach], "ctx", -1)
    g_conv_in = g_ext[:, reach:] + jnp.pad(returned, ((0, 0), (local_len - reach, 0), (0, 0)))
    g_conv_in = g_conv_in.reshape(rows, inner).astype(BF16)
    if fast:
        final, g_normed_part, other = finish_weights(
            x, first, g_conv_in, results[1][0], results[0][1], masks_float[:, :, 0].T, conv_weight, gate_weight
        )
        halves = [jnp.concatenate([final[i], final[i + 1]], axis=1) for i in range(0, 14, 2)]
        gate_grads.append(jnp.stack(halves[:2]))
        conv_grad = jnp.stack([jnp.concatenate([halves[2 + m], halves[4 + m]], axis=1) for m in range(2)])
        out_grads.append(halves[6])
    else:
        conv_grad = summed(terms_of(x[:modes], lax.all_gather(g_conv_in, "shard", axis=0, tiled=True)))
        g_normed_part = sum(
            product(grad * masks[index], weight[index], 1, 1)
            for weight, grad in ((conv_weight, g_conv_in), (gate_weight, g_gate))
            for index in range(modes)
        )
    in_grad = jnp.stack([conv_grad, jnp.concatenate(gate_grads, axis=2)], axis=2)
    out_grad = jnp.concatenate(out_grads, axis=1).T
    group = lax.axis_size("shard") * lax.axis_size("ctx")
    terms = jnp.concatenate(
        [delta_terms.reshape(modes * group, -1, inner), select_terms.reshape(modes * group, -1, inner)], axis=1
    ).astype(BF16)
    terms = terms.reshape(modes, group, -1, inner).transpose(1, 0, 2, 3).reshape(group, -1, inner)
    terms = jnp.pad(terms, ((0, 0), (0, -terms.shape[1] % 16), (0, 0)))
    terms = lax.psum_scatter(terms, ("shard", "ctx"), scatter_dimension=0, tiled=True)[0].astype(jnp.float32)
    deep = rank // group
    terms = terms[: modes * (terms.shape[0] // modes)]
    each = deep + full_select.shape[1] // group
    terms = terms[: modes * each].reshape(modes, each, inner)
    delta_grad, select_grad = terms[:, :deep], terms[:, deep:]

    row_total = pair_total(jnp.sum(g_normed_part * norm_gain * whole, axis=1, keepdims=True))
    gain_part = jnp.sum(g_normed_part * whole * inverse, axis=0)
    scalars = jnp.stack([stream_sq * (1.0 / tps), jnp.sum(mix_local * mix_local), count * (1.0 / tps)])
    small = jnp.concatenate([bias_grad, decay_grad, skip_grad[None], filter_grad, offset_grad[None]], axis=0)
    if fast and width == inner and small.shape[0] == 24:
        wide = jnp.stack([gain_part, jnp.pad(scalars, (0, width - 3))])
        sums = small_sum(jnp.concatenate([small, jnp.pad(wide, ((0, 6), (0, 0)))], axis=0))
        small_total, gain_total, scalars = sums[:24], sums[24], sums[25, :3]
    else:
        small_total = lax.psum(small, ("shard", "ctx"))
        wide = lax.psum(jnp.concatenate([gain_part, scalars]), ("shard", "ctx", "tp"))
        gain_total, scalars = wide[:width], wide[width:]
    start = lax.axis_index("tp") * part_width
    if fast:
        g_normed = lax.dynamic_slice_in_dim(g_normed_part, start, part_width, 1) + other.astype(jnp.float32)
    else:
        g_normed = lax.psum_scatter(
            g_normed_part.astype(BF16), "tp", scatter_dimension=1, tiled=True
        ).astype(jnp.float32)
    own_gain = lax.dynamic_slice_in_dim(norm_gain, start, part_width, 0)
    g_stream = inverse * own_gain * g_normed - local_stream * inverse**3 * row_total / width
    gain_grad = lax.dynamic_slice_in_dim(gain_total, start, part_width, 0)
    upstream_local = upstream.reshape(rows, part_width).astype(jnp.float32)
    stream_gradient = (upstream_local + g_stream).astype(BF16).reshape(seqs, local_len, part_width)

    denominator = jnp.maximum(scalars[2], 1.0) * width
    stream_rms = jnp.sqrt(scalars[0] / denominator)
    mixer_rms = jnp.sqrt(scalars[1] / denominator)
    return (
        output,
        stream_gradient,
        gain_grad,
        in_grad,
        select_grad,
        delta_grad,
        small_total[:modes],
        out_grad,
        small_total[modes + states + 1 : modes + states + 2 + reach],
        small_total[modes + states + 2 + reach],
        small_total[modes : modes + states],
        small_total[modes + states],
        stream_rms,
        mixer_rms,
    )


def solution(mesh):
    return jax.shard_map(
        per_device,
        mesh=mesh,
        in_specs=(
            P("shard", "ctx", "tp"),
            P(),
            P(None, "shard", None, "tp"),
            P(None, "shard", "tp"),
            P(None, "shard", "tp"),
            P(None, "tp"),
            P("tp", "shard"),
            P(None, "tp"),
            P("tp"),
            P(None, "tp"),
            P("tp"),
            P("shard", None),
            P("shard", "ctx"),
            P("shard", "ctx"),
            P("shard", "ctx", "tp"),
        ),
        out_specs=(
            P("shard", "ctx", "tp"),
            P("shard", "ctx", "tp"),
            P("tp"),
            P(None, ("shard", "ctx"), None, "tp"),
            P(None, ("shard", "ctx"), "tp"),
            P(None, ("shard", "ctx"), "tp"),
            P(None, "tp"),
            P("tp", ("shard", "ctx")),
            P(None, "tp"),
            P("tp"),
            P(None, "tp"),
            P("tp"),
            P(),
            P(),
        ),
        check_vma=False,
    )
```

```python
import functools
import jax
import jax.numpy as jnp
from jax import lax
from jax.experimental import pallas as pl
from jax.experimental.pallas import tpu as pltpu

LOG2E = 1.4426950408889634
EPSILON = 1e-05
VMEM_LIMIT = 60 * 1024 * 1024


def sigmoid(value):
    return 1.0 / (1.0 + jnp.exp(-value))


def softplus(value):
    return jnp.maximum(value, 0.0) + jnp.log1p(jnp.exp(-jnp.abs(value)))


def stage_rows(raw_ref, conv_ref, gate_ref, gg_ref, delta_s, conv_s, g_s, groups):
    def step(block, _):
        top = pl.multiple_of(block * 16, 16)
        for group in range(groups):
            lanes = slice(group * 128, group * 128 + 128)
            delta = softplus(raw_ref[pl.ds(top, 16), lanes])
            conv = conv_ref[pl.ds(top, 16), lanes].astype(jnp.float32)
            gate = gate_ref[pl.ds(top, 16), lanes]
            g_mixed = gg_ref[pl.ds(top, 16), lanes] * (gate * sigmoid(gate))
            for part in range(2):
                rows = pl.ds(pl.multiple_of(((block * 2 + part) * groups + group) * 8, 8), 8)
                eight = slice(part * 8, part * 8 + 8)
                delta_s[rows, :] = delta[eight]
                conv_s[rows, :] = conv[eight]
                g_s[rows, :] = g_mixed[eight]
        return 0

    lax.fori_loop(0, raw_ref.shape[0] // 16, step, 0)


def ends_of(first, tokens, groups, states, a_ref, b_ref, c_ref, cut_ref, delta_s, conv_s, g_s):
    def eight_tokens(tile, carry):
        h, p, l = (list(part) for part in carry)
        for i in range(8):
            rows = pl.ds(tile * (groups * 8) + i, groups, stride=8)
            delta = delta_s[rows, :]
            signal = delta * conv_s[rows, :]
            g = g_s[rows, :]
            token = first + tile * 8 + i
            reach = delta + cut_ref[token]
            for n in range(states):
                decay = jnp.exp2(reach * a_ref[n])
                h[n] = decay * h[n] + signal * b_ref[token * states + n]
                p[n] = decay * p[n]
                l[n] = l[n] + p[n] * (g * c_ref[token * states + n])
        return tuple(h), tuple(p), tuple(l)

    zero = tuple(jnp.zeros((groups, 128), jnp.float32) for _ in range(states))
    one = tuple(jnp.ones((groups, 128), jnp.float32) for _ in range(states))
    return lax.fori_loop(0, tokens // 8, eight_tokens, (zero, one, zero))


def ends_kernel(groups, states, raw_ref, conv_ref, gate_ref, gg_ref, a_ref, b_ref, c_ref,
                cut_ref, h_ref, p_ref, l_ref, delta_s, conv_s, g_s):
    tokens = raw_ref.shape[0]
    stage_rows(raw_ref, conv_ref, gate_ref, gg_ref, delta_s, conv_s, g_s, groups)
    h, p, l = ends_of(pl.program_id(0) * tokens, tokens, groups, states, a_ref, b_ref, c_ref, cut_ref,
                      delta_s, conv_s, g_s)
    for n in range(states):
        h_ref[n], p_ref[n], l_ref[n] = h[n], p[n], l[n]


def entering_kernel(groups, states, seqs, raw_ref, conv_ref, gate_ref, gg_ref, a_ref, b_ref, c_ref, cut_ref,
                    normed_ref, gmix_ref, flag_ref, h0_ref, q0_ref, normed_group, gmix_group, flag_group, delta_s,
                    conv_s, g_s, ahead, behind, before, after, up_send, up_recv, down_send, down_recv, row_send,
                    row_recv, stay_sem):
    shard, ctx = lax.axis_index("shard"), lax.axis_index("ctx")
    block, seq = pl.program_id(0), pl.program_id(1)
    step = block * seqs + seq
    steps = ahead.shape[0]
    tokens = raw_ref.shape[0]
    rows, deep = normed_ref.shape[0], normed_ref.shape[1] // 4

    def remote(source, target, send_sem, recv_sem, to):
        return pltpu.make_async_remote_copy(src_ref=source, dst_ref=target, send_sem=send_sem, recv_sem=recv_sem,
                                            device_id=to, device_id_type=MESH)

    def features(owner):
        return pl.ds(pl.multiple_of(owner * deep, deep), deep)

    def from_me():
        mine = pl.ds(pl.multiple_of(shard * rows, rows), rows)
        return normed_group.at[mine], gmix_group.at[mine], flag_group.at[:, mine]

    def row_copies(k):
        peer = lax.rem(shard + k, 4)
        sources = (normed_ref.at[:, features(peer)], gmix_ref.at[:, features(peer)], flag_ref)
        return [remote(s, t, row_send.at[k - 1, i], row_recv.at[k - 1, i], {"shard": peer})
                for i, (s, t) in enumerate(zip(sources, from_me()))]

    def stays():
        sources = (normed_ref.at[:, features(shard)], gmix_ref.at[:, features(shard)], flag_ref)
        return [pltpu.make_async_copy(s, t, stay_sem.at[i]) for i, (s, t) in enumerate(zip(sources, from_me()))]

    def up(i, d):
        return remote(ahead.at[i], before.at[d - 1, i], up_send.at[i, d - 1], up_recv.at[i, d - 1], {"ctx": ctx + d})

    def down(i, d):
        return remote(behind.at[i], after.at[d - 1, i], down_send.at[i, d - 1], down_recv.at[i, d - 1],
                      {"ctx": ctx - d})

    @pl.when(step == 0)
    def _():
        barrier = pltpu.get_barrier_semaphore()
        for k in range(1, 4):
            pl.semaphore_signal(barrier, inc=1, device_id={"shard": lax.rem(shard + k, 4)}, device_id_type=MESH)
            pl.semaphore_signal(barrier, inc=1, device_id={"ctx": lax.rem(ctx + k, 4)}, device_id_type=MESH)
        pl.semaphore_wait(barrier, 6)
        for k in range(1, 4):
            for copy in row_copies(k):
                copy.start()
        for copy in stays():
            copy.start()
        for d in range(1, 4):
            @pl.when(ctx < d)
            def _():
                before[d - 1] = jnp.zeros(before.shape[1:], before.dtype)

            @pl.when(ctx + d > 3)
            def _():
                after[d - 1] = jnp.zeros(after.shape[1:], after.dtype)

    stage_rows(raw_ref, conv_ref, gate_ref, gg_ref, delta_s, conv_s, g_s, groups)
    h, p, l = ends_of(seq * tokens, tokens, groups, states, a_ref, b_ref, c_ref, cut_ref, delta_s, conv_s, g_s)
    for n in range(0, states, 2):
        for k, values in enumerate((h, p)):
            both = jnp.concatenate([values[n], values[n + 1]], axis=0).astype(ahead.dtype)
            ahead[step, k, n * groups : (n + 2) * groups, :] = both
        for k, values in enumerate((l, p)):
            both = jnp.concatenate([values[n], values[n + 1]], axis=0).astype(behind.dtype)
            behind[step, k, n * groups : (n + 2) * groups, :] = both

    for d in range(1, 4):
        @pl.when(ctx + d < 4)
        def _():
            up(step, d).start()

        @pl.when(ctx >= d)
        def _():
            down(step, d).start()

    @pl.when(step == steps - 1)
    def _():
        for d in range(1, 4):
            for i in range(steps):
                @pl.when(ctx >= d)
                def _():
                    up(i, d).wait_recv()
                    down(i, d).wait_send()

                @pl.when(ctx + d < 4)
                def _():
                    up(i, d).wait_send()
                    down(i, d).wait_recv()

        for i in range(steps):
            for out, got in ((h0_ref, before), (q0_ref, after)):
                total = got[2, i, 0].astype(jnp.float32)
                for d in (1, 0):
                    total = got[d, i, 1].astype(jnp.float32) * total + got[d, i, 0].astype(jnp.float32)
                out[i] = total
        for k in range(1, 4):
            for copy in row_copies(k):
                copy.wait()
        for copy in stays():
            copy.wait()


def scan_kernel(groups, states, fsplit, bsplit, raw_ref, conv_ref, gate_ref, gg_ref, skip_ref, a_ref, h0_ref,
                q0_ref, b_ref, c_ref, cut_ref, gated_ref, ggate_ref, graw_ref, gconv_ref,
                ga_ref, gb_ref, gc_ref, gskip_ref, delta_s, conv_s, g_s, y_s, gs_s, h_s):
    tokens = raw_ref.shape[0]
    tiles = tokens // 8
    first = pl.program_id(0) * tokens
    stage_rows(raw_ref, conv_ref, gate_ref, gg_ref, delta_s, conv_s, g_s, groups)
    lane = lax.broadcasted_iota(jnp.int32, (groups, 128), 1)

    def split_sum(total, names, values, i):
        for n, value in zip(names, values):
            total = jnp.where(lane == i * states + n, jnp.sum(value, axis=1, keepdims=True), total)
        return total

    for low in range(0, states, fsplit):
        names = range(low, low + fsplit)

        def forward(tile, h):
            h = list(h)
            gc = jnp.zeros((groups, 128), jnp.float32) if low == 0 else gc_ref[tile]
            for i in range(8):
                rows = pl.ds(tile * (groups * 8) + i, groups, stride=8)
                delta = delta_s[rows, :]
                signal = delta * conv_s[rows, :]
                g = g_s[rows, :]
                token = tile * 8 + i
                at = (first + token) * states
                reach = delta + cut_ref[first + token]
                y = None
                parts = []
                for k, n in enumerate(names):
                    h_s[token, n] = h[k]
                    decay = jnp.exp2(reach * a_ref[n])
                    h[k] = decay * h[k] + signal * b_ref[at + n]
                    term = h[k] * c_ref[at + n]
                    y = term if y is None else y + term
                    parts.append(h[k] * g)
                gc = split_sum(gc, names, parts, i)
                y_s[rows, :] = y if low == 0 else y + y_s[rows, :]
            gc_ref[tile] = gc
            return tuple(h)

        lax.fori_loop(0, tiles, forward, tuple(h0_ref[n] for n in names))

    def between(block, total):
        top = pl.multiple_of(block * 16, 16)
        new = []
        for group in range(groups):
            lanes = slice(group * 128, group * 128 + 128)
            gate = gate_ref[pl.ds(top, 16), lanes]
            sig = sigmoid(gate)
            y, conv, g = (
                jnp.concatenate([ref[pl.ds(pl.multiple_of(((block * 2 + part) * groups + group) * 8, 8), 8), :]
                                 for part in range(2)], axis=0)
                for ref in (y_s, conv_s, g_s)
            )
            mixed = y + skip_ref[:, lanes] * conv
            gated_ref[pl.ds(top, 16), lanes] = (mixed * (gate * sig)).astype(jnp.bfloat16)
            g_gate = gg_ref[pl.ds(top, 16), lanes] * mixed * sig * (1.0 + gate * (1.0 - sig))
            ggate_ref[pl.ds(top, 16), lanes] = g_gate.astype(jnp.bfloat16)
            product = g * conv
            new.append(total[group] + product[:8] + product[8:])
        return tuple(new)

    sums = lax.fori_loop(0, tokens // 16, between,
                         tuple(jnp.zeros((8, 128), jnp.float32) for _ in range(groups)))
    for group in range(groups):
        gskip_ref[:, group * 128:group * 128 + 128] = sums[group]

    for low in range(0, states, bsplit):
        names = range(low, low + bsplit)

        def backward(step, carry):
            q, ga = (list(part) for part in carry)
            tile = tiles - 1 - step
            gb = jnp.zeros((groups, 128), jnp.float32) if low == 0 else gb_ref[tile]
            for i in reversed(range(8)):
                rows = pl.ds(tile * (groups * 8) + i, groups, stride=8)
                delta = delta_s[rows, :]
                conv = conv_s[rows, :]
                signal = delta * conv
                g = g_s[rows, :]
                token = tile * 8 + i
                at = (first + token) * states
                reach = delta + cut_ref[first + token]
                gd = gs = None
                parts = []
                for k, n in enumerate(names):
                    decay = jnp.exp2(reach * a_ref[n])
                    lam = q[k] + g * c_ref[at + n]
                    q[k] = decay * lam
                    w = q[k] * h_s[token, n]
                    ga[k] = ga[k] + w * delta
                    d_term = w * a_ref[n]
                    s_term = lam * b_ref[at + n]
                    gd = d_term if gd is None else gd + d_term
                    gs = s_term if gs is None else gs + s_term
                    parts.append(lam * signal)
                gb = split_sum(gb, names, parts, i)
                y_s[rows, :] = gd if low == 0 else gd + y_s[rows, :]
                gs_s[rows, :] = gs if low == 0 else gs + gs_s[rows, :]
            gb_ref[tile] = gb
            return tuple(q), tuple(ga)

        zero = tuple(jnp.zeros((groups, 128), jnp.float32) for _ in names)
        _, ga = lax.fori_loop(0, tiles, backward, (tuple(q0_ref[n] for n in names), zero))
        for k, n in enumerate(names):
            ga_ref[n] = ga[k]

    def after(block, _):
        top = pl.multiple_of(block * 16, 16)
        for group in range(groups):
            lanes = slice(group * 128, group * 128 + 128)
            raw = raw_ref[pl.ds(top, 16), lanes]
            gd, gs, conv, delta, g = (
                jnp.concatenate([ref[pl.ds(pl.multiple_of(((block * 2 + part) * groups + group) * 8, 8), 8), :]
                                 for part in range(2)], axis=0)
                for ref in (y_s, gs_s, conv_s, delta_s, g_s)
            )
            g_delta = gd * (1.0 / LOG2E) + conv * gs
            graw_ref[pl.ds(top, 16), lanes] = (g_delta * sigmoid(raw)).astype(jnp.bfloat16)
            gconv_ref[pl.ds(top, 16), lanes] = skip_ref[:, lanes] * g + delta * gs
        return 0

    lax.fori_loop(0, tokens // 16, after, 0)


def sizes(raw, seqs, states):
    rows, inner = raw.shape
    groups = min(8, inner // 128)
    return rows // seqs, inner // (groups * 128), groups


def state_form(value, blocks, groups):
    states = value.shape[0]
    return value.reshape(states, blocks, groups, 128).transpose(1, 0, 2, 3)


def from_state_form(value):
    blocks, states, groups, lanes = value.shape
    return value.transpose(1, 0, 2, 3).reshape(states, blocks * groups * lanes)


def token_spec(tokens, width, block):
    return pl.BlockSpec((tokens, width), lambda s: (s, block))


def state_spec(states, groups):
    return pl.BlockSpec((None, states, groups, 128), lambda s: (s, 0, 0, 0))


def scan_ends(raw, conv, gate, gg, a2, b, c, cut, seqs, block):
    states, groups, _ = a2.shape
    tokens = raw.shape[0] // seqs
    width = groups * 128
    smem = pl.BlockSpec(memory_space=pltpu.SMEM)
    out = jax.ShapeDtypeStruct((seqs, states, groups, 128), jnp.float32)
    elements = raw.shape[0] * width * states
    return pl.pallas_call(
        functools.partial(ends_kernel, groups, states),
        grid=(seqs,),
        in_specs=[token_spec(tokens, width, block)] * 4
        + [pl.BlockSpec((states, groups, 128), lambda s: (0, 0, 0)), smem, smem, smem],
        out_specs=[state_spec(states, groups)] * 3,
        out_shape=[out] * 3,
        scratch_shapes=[pltpu.VMEM((tokens * groups, 128), jnp.float32)] * 3,
        compiler_params=pltpu.CompilerParams(vmem_limit_bytes=VMEM_LIMIT),
        cost_estimate=pl.CostEstimate(flops=8 * elements, bytes_accessed=elements, transcendentals=elements),
        name="scan_ends",
    )(raw, conv, gate, gg, a2, b.reshape(-1), c.reshape(-1), cut.reshape(-1))


def scan_both(raw, conv, gate, gg, skip, a2, h0, q0, b, c, cut, seqs, block):
    states, groups, _ = a2.shape
    rows, inner = raw.shape
    tokens = rows // seqs
    width = groups * 128
    smem = pl.BlockSpec(memory_space=pltpu.SMEM)
    elements = rows * width * states
    token = token_spec(tokens, width, block)
    tiles = tokens // 8
    own = pl.BlockSpec((tokens, width), lambda s: (s, 0))
    pair = pl.BlockSpec((tiles, groups, 128), lambda s: (s, 0, 0))
    pair_shape = jax.ShapeDtypeStruct((rows // 8, groups, 128), jnp.float32)
    low = jax.ShapeDtypeStruct((rows, width), jnp.bfloat16)
    return pl.pallas_call(
        functools.partial(scan_kernel, groups, states, states, states),
        grid=(seqs,),
        in_specs=[token] * 4
        + [pl.BlockSpec((1, width), lambda s: (0, block)),
           pl.BlockSpec((states, groups, 128), lambda s: (0, 0, 0)),
           state_spec(states, groups), state_spec(states, groups), smem, smem, smem],
        out_specs=[own] * 4 + [state_spec(states, groups), pair, pair,
                               pl.BlockSpec((None, 8, width), lambda s: (s, 0, 0))],
        out_shape=[low, low, low, jax.ShapeDtypeStruct((rows, width), jnp.float32),
                   jax.ShapeDtypeStruct((seqs, states, groups, 128), jnp.float32),
                   pair_shape, pair_shape, jax.ShapeDtypeStruct((seqs, 8, width), jnp.float32)],
        scratch_shapes=[pltpu.VMEM((tokens * groups, 128), jnp.float32)] * 5
        + [pltpu.VMEM((tokens, states, groups, 128), jnp.float32)],
        compiler_params=pltpu.CompilerParams(vmem_limit_bytes=VMEM_LIMIT),
        cost_estimate=pl.CostEstimate(flops=22 * elements, bytes_accessed=2 * elements, transcendentals=2 * elements),
        name="scan_both",
    )(raw, conv, gate, gg, skip.reshape(1, inner), a2, h0, q0, b.reshape(-1), c.reshape(-1), cut.reshape(-1))


def pair_sum(value, states):
    return jnp.sum(value, axis=1).reshape(-1, states)


MESH = pl.DeviceIdType.MESH


def front_kernel(in_ref, out_ref, stream_ref, gain_ref, mask_ref, conv_full, gate_full, out_full, conv_in, gate_in,
                 normed_ref, whole_ref, conv_s, rows_s, weight_s, theirs, x_sem, load_sem, stay_sem, core_send,
                 core_recv, y_send, y_recv, z_send, z_recv, pass_send, pass_recv, rest_send, rest_recv):
    shard, ctx, tp = lax.axis_index("shard"), lax.axis_index("ctx"), lax.axis_index("tp")
    near, far, beyond = shard + 1 - 2 * lax.rem(shard, 2), lax.rem(shard + 2, 4), 3 - shard
    core, across, beside = {"shard": near}, {"shard": far}, {"tp": 1 - tp}
    side = {"ctx": ctx + 1 - 2 * lax.rem(ctx, 2)}
    half = lax.rem(ctx, 2)
    kinds, modes, depth, inner = in_ref.shape
    columns = out_ref.shape[1]
    tokens, part_width = stream_ref.shape
    width = 2 * part_width
    piece, piece_out = depth // 4, out_ref.shape[0] // 4
    inside = kinds * modes * 2
    chunks = inside + 2
    fulls = (conv_full, gate_full)
    totals = (conv_s, gate_in)

    barrier = pltpu.get_barrier_semaphore()
    for peer in (core, across, side, beside):
        pl.semaphore_signal(barrier, inc=1, device_id=peer, device_id_type=MESH)
    pl.semaphore_wait(barrier, 4)

    def remote(source, target, send_sem, recv_sem, to):
        return pltpu.make_async_remote_copy(src_ref=source, dst_ref=target, send_sem=send_sem, recv_sem=recv_sem,
                                            device_id=to, device_id_type=MESH)

    def span(start, count):
        return pl.ds(pl.multiple_of(start, count), count)

    def view(owner, part, c):
        if c < inside:
            rows = span(owner * depth + (part * 2 + c % 2) * piece, piece)
            return fulls[c // (2 * modes)].at[c // 2 % modes, rows]
        return out_full.at[span((part * 2 + c - inside) * piece_out, piece_out), span(owner * columns, columns)]

    def own(part, c):
        if c < inside:
            return in_ref.at[c // (2 * modes), c // 2 % modes, span((part * 2 + c % 2) * piece, piece)]
        return out_ref.at[span((part * 2 + c - inside) * piece_out, piece_out), :]

    def cross(c):
        return remote(own(half, c), view(shard, half, c), y_send.at[c], y_recv.at[c], across)

    def onward(c):
        return remote(view(far, half, c), view(far, half, c), z_send.at[c], z_recv.at[c], side)

    def passed(c):
        return remote(view(far, half, c), view(far, half, c), pass_send.at[c], pass_recv.at[c], core)

    def rest(c):
        return remote(view(far, 1 - half, c), view(far, 1 - half, c), rest_send.at[c], rest_recv.at[c], core)

    def place(h, m):
        return fulls[h].at[m, span(shard * depth, depth)]

    def to_core(i):
        if i < kinds * modes:
            h, m = i // modes, i % modes
            return remote(in_ref.at[h, m], place(h, m), core_send.at[i], core_recv.at[i], core)
        return remote(out_ref, out_full.at[:, span(shard * columns, columns)], core_send.at[i], core_recv.at[i], core)

    def load(source, slot, count):
        return pltpu.make_async_copy(source, weight_s.at[slot, pl.ds(0, count)], load_sem.at[slot])

    def multiply(h, m, start, count, slot, fresh=False):
        rows = rows_s[m, :, span(start, count)]

        def tile(j, _):
            lanes = span(j * 256, 256)
            term = jnp.dot(rows, weight_s[slot, :count, lanes], preferred_element_type=jnp.float32)
            totals[h][:, lanes] = term if fresh else totals[h][:, lanes] + term
            return 0

        lax.fori_loop(0, inner // 256, tile, 0)

    def run(blocks):
        load(blocks[0][4], 0, blocks[0][3]).start()
        for i, (h, m, start, count, source) in enumerate(blocks):
            if i + 1 < len(blocks):
                load(blocks[i + 1][4], (i + 1) % 2, blocks[i + 1][3]).start()
            load(source, i % 2, count).wait()
            multiply(h, m, start, count, i % 2)

    def own_shard():
        for i in range(kinds * modes):
            h, m = i // modes, i % modes
            load(in_ref.at[h, m], i % 2, depth).start()
            load(in_ref.at[h, m], i % 2, depth).wait()
            stay = pltpu.make_async_copy(weight_s.at[i % 2], place(h, m), stay_sem.at[0])
            stay.start()
            multiply(h, m, shard * depth, depth, i % 2, fresh=m == 0)
            stay.wait()

    def near_shard():
        for i in range(kinds * modes):
            to_core(i).wait_recv()
        run([(i // modes, i % modes, near * depth, depth,
              fulls[i // modes].at[i % modes, span(near * depth, depth)]) for i in range(kinds * modes)])

    def quarter(i, owner, part):
        h, m = i // modes, i % modes
        start = owner * depth + part * (depth // 2)
        return h, m, start, depth // 2, fulls[h].at[m, span(start, depth // 2)]

    def direct(i):
        for c in (2 * i, 2 * i + 1):
            passed(c).wait_recv()
        run([quarter(i, far, half), quarter(i, beyond, half)])

    def relayed(i):
        for c in (2 * i, 2 * i + 1):
            rest(c).wait_recv()
        run([quarter(i, far, 1 - half), quarter(i, beyond, 1 - half)])

    def normed_rows():
        mine, other = span(tp * part_width, part_width), span((1 - tp) * part_width, part_width)

        def block(i, _):
            rows = span(i * 16, 16)
            left = stream_ref[rows, :].astype(jnp.float32)
            right = theirs[rows, :].astype(jnp.float32)
            square = jnp.sum(left * left, axis=1, keepdims=True) + jnp.sum(right * right, axis=1, keepdims=True)
            inverse = lax.rsqrt(square * (1.0 / width) + EPSILON)
            for lanes, value in ((mine, left), (other, right)):
                whole_ref[rows, lanes] = value.astype(whole_ref.dtype)
                result = (value * inverse * gain_ref[:, lanes]).astype(normed_ref.dtype)
                normed_ref[rows, lanes] = result
                for m in range(modes):
                    masked = result.astype(jnp.float32) * mask_ref[rows, m : m + 1]
                    rows_s[m, rows, lanes] = masked.astype(rows_s.dtype)
            return 0

        lax.fori_loop(0, tokens // 16, block, 0)

    across_tp = remote(stream_ref, theirs, x_sem.at[0], x_sem.at[1], beside)
    across_tp.start()
    cross(0).start()
    cross(1).start()
    stay_out = pltpu.make_async_copy(out_ref, out_full.at[:, span(shard * columns, columns)], stay_sem.at[1])
    stay_out.start()
    for i in range(kinds * modes + 1):
        to_core(i).start()

    work = {2: [own_shard], 3: [near_shard], 4: [lambda: direct(0)], 5: [lambda: relayed(0), lambda: direct(1)],
            6: [lambda: relayed(1)], 7: [lambda: direct(2)], 8: [lambda: relayed(2)],
            9: [lambda: direct(3), lambda: relayed(3)]}
    for c in range(chunks):
        cross(c).wait()
        if c + 2 < chunks:
            cross(c + 2).start()
        onward(c).start()
        passed(c).start()
        if c:
            onward(c - 1).wait_recv()
            rest(c - 1).start()
        if c == 1:
            across_tp.wait()
            normed_rows()
        for task in work.get(c, []):
            task()
    onward(chunks - 1).wait_recv()
    rest(chunks - 1).start()

    def cast(i, _):
        rows = span(i * 16, 16)
        conv_in[rows, :] = conv_s[rows, :].astype(conv_in.dtype)
        return 0

    lax.fori_loop(0, tokens // 16, cast, 0)
    stay_out.wait()
    to_core(kinds * modes).wait_recv()
    for i in range(kinds * modes + 1):
        to_core(i).wait_send()
    for c in range(chunks):
        if c >= inside:
            passed(c).wait_recv()
            rest(c).wait_recv()
        onward(c).wait_send()
        passed(c).wait_send()
        rest(c).wait_send()


def front(in_own, out_own, stream, gain, masks):
    kinds, modes, depth, inner = in_own.shape
    tokens, part_width = stream.shape
    width = gain.shape[0]
    chunks = kinds * modes * 2 + 2
    any_space = pl.BlockSpec(memory_space=pl.ANY)
    vmem = pl.BlockSpec(memory_space=pltpu.VMEM)
    many = pltpu.SemaphoreType.DMA((chunks,))
    two = pltpu.SemaphoreType.DMA((2,))
    five = pltpu.SemaphoreType.DMA((kinds * modes + 1,))
    full = jax.ShapeDtypeStruct((modes, 4 * depth, inner), in_own.dtype)
    low = jax.ShapeDtypeStruct((tokens, width), jnp.bfloat16)
    return pl.pallas_call(
        front_kernel,
        in_specs=[any_space] + [vmem] * 4,
        out_specs=[any_space] * 3 + [vmem] * 4,
        out_shape=[full, full, jax.ShapeDtypeStruct((inner, 4 * out_own.shape[1]), out_own.dtype),
                   jax.ShapeDtypeStruct((tokens, inner), jnp.bfloat16),
                   jax.ShapeDtypeStruct((tokens, inner), jnp.float32), low, low],
        scratch_shapes=[pltpu.VMEM((tokens, inner), jnp.float32), pltpu.VMEM((modes, tokens, width), jnp.bfloat16),
                        pltpu.VMEM((2, depth, inner), jnp.bfloat16), pltpu.VMEM(stream.shape, jnp.bfloat16)]
        + [two] * 3 + [five] * 2 + [many] * 8,
        compiler_params=pltpu.CompilerParams(collective_id=1, has_side_effects=True, vmem_limit_bytes=VMEM_LIMIT),
        cost_estimate=pl.CostEstimate(flops=0, bytes_accessed=400_000_000, transcendentals=0),
        name="front",
    )(in_own, out_own, stream, gain.reshape(1, width), masks)


def finish_kernel(x_ref, first_0, first_1, first_2, first_3, conv_ref, gated_ref, gate_ref, mask_ref, conv_weight,
                  gate_weight, sum_ref, normed_ref, other_ref, blocks, part, came, gate_s, weight_s, give_s, y_send,
                  y_recv, core_send, core_recv, pass_send, pass_recv, local_sem, first_sem, gate_sem, weight_sem,
                  x_sem, up_send, up_recv, down_send, down_recv):
    shard, ctx, tp = lax.axis_index("shard"), lax.axis_index("ctx"), lax.axis_index("tp")
    far = lax.rem(shard + 2, 4)
    core = {"shard": shard + 1 - 2 * lax.rem(shard, 2)}
    across = {"shard": far}
    jobs, units, last = blocks.shape[0], part.shape[0], 3
    tokens, width = gated_ref.shape
    deep, narrow = sum_ref.shape[1:]
    up, down, beside = {"ctx": ctx + 1}, {"ctx": ctx - 1}, {"tp": 1 - tp}
    features = weight_s.shape[3]
    steps = normed_ref.shape[1] // features

    barrier = pltpu.get_barrier_semaphore()
    for peer in (core, across, beside):
        pl.semaphore_signal(barrier, inc=1, device_id=peer, device_id_type=MESH)

    @pl.when(ctx < last)
    def _():
        pl.semaphore_signal(barrier, inc=1, device_id=up, device_id_type=MESH)

    @pl.when(ctx > 0)
    def _():
        pl.semaphore_signal(barrier, inc=1, device_id=down, device_id_type=MESH)

    pl.semaphore_wait(barrier, 3 + jnp.where(ctx < last, 1, 0) + jnp.where(ctx > 0, 1, 0))

    sources = [None, conv_ref.at[:, pl.ds(0, width)], conv_ref.at[:, pl.ds(width, width)], gated_ref]

    def rows_of(owner):
        return pl.ds(pl.multiple_of(owner * tokens, tokens), tokens)

    def remote(source, target, send_sem, recv_sem, to):
        return pltpu.make_async_remote_copy(src_ref=source, dst_ref=target, send_sem=send_sem, recv_sem=recv_sem,
                                            device_id=to, device_id_type=MESH)

    def cross(j):
        return remote(sources[j], blocks.at[j, rows_of(shard)], y_send.at[j], y_recv.at[j], across)

    def pair(j):
        return remote(sources[j], blocks.at[j, rows_of(shard)], core_send.at[j], core_recv.at[j], core)

    def onward(j):
        held = blocks.at[j, rows_of(far)]
        return remote(held, held, pass_send.at[j], pass_recv.at[j], core)

    def stay(j):
        return pltpu.make_async_copy(sources[j], blocks.at[j, rows_of(shard)], local_sem.at[j])

    def advance(j):
        cross(j).wait()
        onward(j).start()
        if j + 2 < jobs:
            cross(j + 2).start()

    def hop(u, k, slot, send_sem, recv_sem, to):
        rows = pl.ds(pl.multiple_of(k * deep, deep), deep)
        there = pl.ds(pl.multiple_of(slot * deep, deep), deep)
        return remote(part.at[u, rows], came.at[u, there], send_sem.at[u, k], recv_sem.at[u, k], to)

    def going_up(u, k):
        return hop(u, k, k, up_send, up_recv, up)

    def going_down(u, k):
        return hop(u, k, jnp.where(k == ctx - 1, last + 1, k), down_send, down_recv, down)

    def coming_down(u, k):
        return hop(u, k, jnp.where(k == ctx, last + 1, k), down_send, down_recv, down)

    def add(u, k):
        rows = pl.ds(k * deep, deep)
        total = part[u, rows, :].astype(jnp.float32) + came[u, rows, :].astype(jnp.float32)
        part[u, rows, :] = total.astype(part.dtype)

    def feature_rows(i):
        return pl.multiple_of(lax.rem(i + (1 - tp) * (steps // 2), steps) * features, features)

    def load(i, slot):
        rows = pl.ds(feature_rows(i), features)
        return [pltpu.make_async_copy(ref.at[:, rows], weight_s.at[slot, k], weight_sem.at[slot, k])
                for k, ref in enumerate((conv_weight, gate_weight))]

    def beside_copy():
        return remote(give_s, other_ref, x_sem.at[0], x_sem.at[1], beside)

    owners = (shard, shard + 1 - 2 * lax.rem(shard, 2), far, 3 - shard)
    firsts = [pltpu.make_async_copy(ref, blocks.at[0, rows_of(owner)], first_sem.at[k])
              for k, (owner, ref) in enumerate(zip(owners, (first_0, first_1, first_2, first_3)))]
    for copy in firsts:
        copy.start()
    for j in range(1, min(3, jobs)):
        cross(j).start()
    own_gate = pltpu.make_async_copy(gate_ref, gate_s, gate_sem.at[0])
    own_gate.start()
    for j in range(1, jobs):
        stay(j).start()
        pair(j).start()
    for copy in load(0, 0):
        copy.start()
    for copy in firsts:
        copy.wait()
    own_gate.wait()
    for j in range(1, jobs):
        stay(j).wait()

    def step(t, _):
        for j in range(1, jobs):
            @pl.when(t == 4 * j)
            def _():
                pair(j).wait()
                onward(j).wait()

        @pl.when(t < units)
        def _():
            job = t // 4
            which = jnp.where(t >= 4 * (jobs - 1), 2, lax.rem(t // 2, 2))
            column = lax.rem(t, 2) * narrow
            for c in range(narrow // 256):
                lanes = pl.ds(pl.multiple_of(column + c * 256, 256), 256)
                part[t, :, c * 256 : c * 256 + 256] = jnp.dot(
                    x_ref[which], blocks[job, :, lanes], preferred_element_type=jnp.float32
                ).astype(part.dtype)

        u = t - ctx

        @pl.when((u >= 0) & (u < units))
        def _():
            for k in range(last, 0, -1):
                @pl.when(k > ctx)
                def _():
                    @pl.when(ctx > 0)
                    def _():
                        going_up(u, k).wait_recv()
                        add(u, k)

                    going_up(u, k).start()

        v = t - (last - ctx)

        @pl.when((v >= 0) & (v < units))
        def _():
            for k in range(last):
                @pl.when(k < ctx)
                def _():
                    @pl.when(ctx < last)
                    def _():
                        coming_down(v, k).wait_recv()
                        add(v, k)

                    going_down(v, k).start()

        @pl.when(t < steps)
        def _():
            slot = lax.rem(t, 2)

            @pl.when(t + 1 < steps)
            def _():
                for copy in load(t + 1, 1 - slot):
                    copy.start()

            for copy in load(t, slot):
                copy.wait()
            mine = rows_of(shard)
            left = (blocks[1, mine, :], blocks[2, mine, :], gate_s[...], blocks[0, mine, :])
            total = None
            for k, rows in enumerate(left):
                weight = weight_s[slot, k // 2, :, :, (k % 2) * width : (k % 2) * width + width]
                term = lax.dot_general(rows, weight.reshape(2 * features, width), (((1,), (1,)), ((), ())),
                                       preferred_element_type=jnp.float32)
                total = term if total is None else total + term
            total = mask_ref[:, 0:1] * total[:, :features] + mask_ref[:, 1:2] * total[:, features:]
            at = feature_rows(t)
            normed_ref[:, pl.ds(at, features)] = total

            @pl.when(t < steps // 2)
            def _():
                give_s[:, pl.ds(pl.multiple_of(t * features, features), features)] = total.astype(give_s.dtype)

            @pl.when(t == steps // 2)
            def _():
                beside_copy().start()

        w = t - last

        @pl.when(w >= 0)
        def _():
            rows = pl.ds(pl.multiple_of(ctx * deep, deep), deep)
            sum_ref[w] = part[w, rows, :].astype(jnp.float32)

            @pl.when(ctx > 0)
            def _():
                going_up(w, ctx).wait_recv()
                sum_ref[w] += came[w, rows, :].astype(jnp.float32)

            @pl.when(ctx < last)
            def _():
                coming_down(w, ctx).wait_recv()
                sum_ref[w] += came[w, (last + 1) * deep :, :].astype(jnp.float32)

        for j in range(1, jobs):
            @pl.when(t == 4 * j - 2)
            def _():
                advance(j)

        return 0

    lax.fori_loop(0, units + last, step, 0)
    beside_copy().wait()

    def drain(u, _):
        for k in range(last + 1):
            @pl.when(k > ctx)
            def _():
                going_up(u, k).wait_send()

            @pl.when(k < ctx)
            def _():
                going_down(u, k).wait_send()

        return 0

    lax.fori_loop(0, units, drain, 0)


def finish_weights(x, first, g_conv_in, gated, g_gate, masks, conv_weight, gate_weight):
    _, features, group = x.shape
    tokens, width = gated.shape
    jobs, units, narrow = 4, 14, width // 2
    deep = features // 4
    total = conv_weight.shape[1]
    any_space = pl.BlockSpec(memory_space=pl.ANY)
    vmem = pl.BlockSpec(memory_space=pltpu.VMEM)
    sums = pltpu.SemaphoreType.DMA((units, 4))
    job_sems = pltpu.SemaphoreType.DMA((jobs,))
    two = pltpu.SemaphoreType.DMA((2,))
    flops = 2 * units * features * group * narrow + 8 * tokens * total * 2 * width * 2
    return pl.pallas_call(
        finish_kernel,
        in_specs=[vmem] + [any_space] * 7 + [vmem] + [any_space] * 2,
        out_specs=[vmem] * 3,
        out_shape=[jax.ShapeDtypeStruct((units, deep, narrow), jnp.float32),
                   jax.ShapeDtypeStruct((tokens, total), jnp.float32),
                   jax.ShapeDtypeStruct((tokens, total // 2), jnp.bfloat16)],
        scratch_shapes=[pltpu.VMEM((jobs, group, width), jnp.bfloat16),
                        pltpu.VMEM((units, features, narrow), jnp.bfloat16),
                        pltpu.VMEM((units, 5 * deep, narrow), jnp.bfloat16),
                        pltpu.VMEM((tokens, width), jnp.bfloat16),
                        pltpu.VMEM((2, 2, 2, 128, 2 * width), jnp.bfloat16),
                        pltpu.VMEM((tokens, total // 2), jnp.bfloat16)]
        + [job_sems] * 8 + [two, pltpu.SemaphoreType.DMA((2, 2)), two] + [sums] * 4,
        compiler_params=pltpu.CompilerParams(collective_id=2, has_side_effects=True, vmem_limit_bytes=VMEM_LIMIT),
        cost_estimate=pl.CostEstimate(flops=flops, bytes_accessed=500_000_000, transcendentals=0),
        name="finish_weights",
    )(x, *first, g_conv_in, gated, g_gate, masks, conv_weight, gate_weight)


def scan_entering(raw, conv, gate, gg, a2, b, c, cut, normed, g_mix, flags, seqs):
    blocks, states, groups, _ = a2.shape
    rows = raw.shape[0]
    tokens = rows // seqs
    width = groups * 128
    steps = blocks * seqs
    smem = pl.BlockSpec(memory_space=pltpu.SMEM)
    any_space = pl.BlockSpec(memory_space=pl.ANY)
    vmem = pl.BlockSpec(memory_space=pltpu.VMEM)
    token = pl.BlockSpec((tokens, width), lambda j, s: (s, j))
    elements = raw.size * states
    ends = pltpu.VMEM((steps, 2, states * groups, 128), jnp.bfloat16)
    came = pltpu.VMEM((3, steps, 2, states * groups, 128), jnp.bfloat16)
    sums = pltpu.SemaphoreType.DMA((steps, 3))
    nine = pltpu.SemaphoreType.DMA((3, 3))
    state = jax.ShapeDtypeStruct((steps, states * groups, 128), jnp.float32)
    group = jax.ShapeDtypeStruct((4 * rows, normed.shape[1] // 4), jnp.bfloat16)
    h0, q0, *lists = pl.pallas_call(
        functools.partial(entering_kernel, groups, states, seqs),
        grid=(blocks, seqs),
        in_specs=[token] * 4
        + [pl.BlockSpec((None, states, groups, 128), lambda j, s: (j, 0, 0, 0)), smem, smem, smem]
        + [any_space] * 3,
        out_specs=[vmem] * 2 + [any_space] * 3,
        out_shape=[state, state, group, group, jax.ShapeDtypeStruct((flags.shape[0], 4 * rows), jnp.bfloat16)],
        scratch_shapes=[pltpu.VMEM((tokens * groups, 128), jnp.float32)] * 3 + [ends] * 2 + [came] * 2
        + [sums] * 4 + [nine] * 2 + [pltpu.SemaphoreType.DMA((3,))],
        compiler_params=pltpu.CompilerParams(collective_id=4, has_side_effects=True, vmem_limit_bytes=VMEM_LIMIT),
        cost_estimate=pl.CostEstimate(flops=8 * elements, bytes_accessed=elements, transcendentals=elements),
        name="scan_entering",
    )(raw, conv, gate, gg, a2, b.reshape(-1), c.reshape(-1), cut.reshape(-1), normed, g_mix, flags)
    shape = (blocks, seqs, states, groups, 128)
    return h0.reshape(shape), q0.reshape(shape), lists


def small_kernel(in_ref, out_ref, x_in, mine, y_in, z_in, x_sem, a_send, a_recv, b_send, b_recv, c_send, c_recv):
    shard, ctx, tp = lax.axis_index("shard"), lax.axis_index("ctx"), lax.axis_index("tp")
    quarter = out_ref.shape[0] // 4
    other = {"tp": 1 - tp}

    def shard_peer(k):
        return {"shard": lax.rem(shard + k, 4)}

    def ctx_peer(k):
        return {"ctx": lax.rem(ctx + k, 4)}

    barrier = pltpu.get_barrier_semaphore()
    pl.semaphore_signal(barrier, inc=1, device_id=other, device_id_type=MESH)
    for k in range(1, 4):
        pl.semaphore_signal(barrier, inc=1, device_id=shard_peer(k), device_id_type=MESH)
        pl.semaphore_signal(barrier, inc=1, device_id=ctx_peer(k), device_id_type=MESH)
    pl.semaphore_wait(barrier, 7)

    def remote(source, target, send_sem, recv_sem, to):
        copy = pltpu.make_async_remote_copy(src_ref=source, dst_ref=target, send_sem=send_sem, recv_sem=recv_sem,
                                            device_id=to, device_id_type=MESH)
        copy.start()
        return copy

    def rows_of(k):
        return pl.ds(pl.multiple_of(k * quarter, 8), quarter)

    total = in_ref.shape[0]
    copy = remote(in_ref.at[pl.ds(total - 8, 8)], x_in, x_sem.at[0], x_sem.at[1], other)
    mine[...] = in_ref[...]
    copy.wait()
    mine[total - 8 :, :] = in_ref[total - 8 :, :] + x_in[...]

    copies = [remote(mine.at[rows_of(lax.rem(shard + k, 4))], y_in.at[k - 1], a_send.at[k - 1], a_recv.at[k - 1],
                     shard_peer(k)) for k in range(1, 4)]
    for copy in copies:
        copy.wait()
    z_in[ctx] = mine[rows_of(shard), :] + y_in[0] + y_in[1] + y_in[2]
    copies = [remote(z_in.at[ctx], z_in.at[ctx], b_send.at[k - 1], b_recv.at[k - 1], ctx_peer(k))
              for k in range(1, 4)]
    for copy in copies:
        copy.wait()
    out_ref[rows_of(shard), :] = (z_in[0] + z_in[1]) + (z_in[2] + z_in[3])
    copies = [remote(out_ref.at[rows_of(shard)], out_ref.at[rows_of(shard)], c_send.at[k - 1], c_recv.at[k - 1],
                     shard_peer(k)) for k in range(1, 4)]
    for copy in copies:
        copy.wait()


def small_sum(value):
    rows, width = value.shape
    quarter = rows // 4
    vmem = pl.BlockSpec(memory_space=pltpu.VMEM)
    three = pltpu.SemaphoreType.DMA((3,))
    return pl.pallas_call(
        small_kernel,
        in_specs=[vmem],
        out_specs=vmem,
        out_shape=jax.ShapeDtypeStruct(value.shape, value.dtype),
        scratch_shapes=[pltpu.VMEM((8, width), value.dtype), pltpu.VMEM(value.shape, value.dtype),
                        pltpu.VMEM((3, quarter, width), value.dtype), pltpu.VMEM((4, quarter, width), value.dtype),
                        pltpu.SemaphoreType.DMA((2,))] + [three] * 6,
        compiler_params=pltpu.CompilerParams(collective_id=3, has_side_effects=True, vmem_limit_bytes=32 * 2**20),
        cost_estimate=pl.CostEstimate(flops=0, bytes_accessed=40_000_000, transcendentals=0),
        name="small_sum",
    )(value)


from jax.sharding import PartitionSpec as P

BF16 = jnp.bfloat16


def from_behind(value, axis, by):
    devices = lax.axis_size(axis)
    pairs = [(i, i + by) for i in range(devices) if 0 <= i + by < devices]
    return lax.ppermute(value, axis, pairs)


def product(left, right, left_dim, right_dim):
    return lax.dot_general(
        left, right, (((left_dim,), (right_dim,)), ((), ())), preferred_element_type=jnp.float32
    )


def exchange_ends(last, total, back, axis):
    devices = lax.axis_size(axis)
    state, adjoint = jnp.zeros_like(last), jnp.zeros_like(last)
    ahead = jnp.stack([last, total]).astype(BF16)
    behind = jnp.stack([back, total]).astype(BF16)
    before = [from_behind(ahead, axis, k) for k in range(1, devices)]
    after = [from_behind(behind, axis, -k) for k in range(1, devices)]
    for part in reversed(before):
        state = part[1].astype(jnp.float32) * state + part[0].astype(jnp.float32)
    for part in reversed(after):
        adjoint = part[1].astype(jnp.float32) * adjoint + part[0].astype(jnp.float32)
    return state, adjoint


def group_rows(normed, g_mix, masks):
    both = lax.all_to_all(jnp.stack([normed, g_mix]), "shard", 2, 1, tiled=True)
    flags = lax.all_gather(masks, "shard", axis=1, tiled=True)
    return jnp.stack([(both[0] * flag[:, None]).T for flag in flags] + [both[1].T])


def per_device(
    stream,
    norm_gain,
    in_weight,
    select_weight,
    delta_weight,
    delta_bias,
    out_weight,
    filter_weight,
    filter_bias,
    decay_log,
    skip_gain,
    segments,
    modality,
    valid,
    upstream,
):
    seqs, local_len, part_width = stream.shape
    width = norm_gain.shape[0]
    inner = out_weight.shape[0]
    states = decay_log.shape[0]
    reach = filter_weight.shape[0] - 1
    rows = seqs * local_len
    tps = lax.axis_size("tp")
    modes, depth = in_weight.shape[:2]
    in_own = in_weight.transpose(2, 0, 1, 3)
    fast = (lax.axis_size("shard"), lax.axis_size("ctx"), lax.axis_size("tp")) == (4, 4, 2)
    if not fast:
        conv_weight, gate_weight = lax.all_gather(in_own, "shard", axis=2, tiled=True)
        full_out = lax.all_gather(out_weight, "shard", axis=1, tiled=True)
    full_select = lax.all_gather(select_weight, "shard", axis=1, tiled=True)
    full_delta = lax.all_gather(delta_weight, "shard", axis=1, tiled=True)
    rank = full_delta.shape[1]
    mode_rows = modality.reshape(rows)
    masks = jnp.stack([(mode_rows == index).astype(BF16)[:, None] for index in range(modes)])
    masks_float = masks.astype(jnp.float32)
    valid_rows = valid.reshape(rows, 1).astype(jnp.float32)

    def apply_modes(values, weights, weight_dim):
        total = product(values * masks[0], weights[0], 1, weight_dim)
        for index in range(1, modes):
            total = total + product(values * masks[index], weights[index], 1, weight_dim)
        return total

    def pair_total(value):
        if tps != 2:
            return lax.psum(value, "tp")
        return value + lax.ppermute(value, "tp", [(0, 1), (1, 0)])

    def half_total(sent, value):
        if tps != 2:
            return lax.psum_scatter(sent, "tp", scatter_dimension=1, tiled=True).astype(jnp.float32)
        own = lax.axis_index("tp") * part_width
        gift = lax.dynamic_slice_in_dim(sent, part_width - own, part_width, 1)
        gift = lax.ppermute(gift, "tp", [(0, 1), (1, 0)])
        return lax.dynamic_slice_in_dim(value, own, part_width, 1) + gift.astype(jnp.float32)

    def modal_terms(values, grads):
        return jnp.stack([product(values * masks[index], grads, 0, 0) for index in range(modes)])

    g_mix = lax.all_gather(upstream, "tp", axis=2, tiled=True).reshape(rows, width) * valid_rows.astype(BF16)

    if fast:
        conv_weight, gate_weight, full_out, conv_in, gate_in, normed, whole = front(
            in_own, out_weight, stream.reshape(rows, part_width), norm_gain, masks_float[:, :, 0].T
        )
        whole = whole.astype(jnp.float32)
    else:
        whole = lax.all_gather(stream, "tp", axis=2, tiled=True).reshape(rows, width).astype(jnp.float32)
    inverse = lax.rsqrt(jnp.mean(whole * whole, axis=1, keepdims=True) + EPSILON)
    if not fast:
        normed = (whole * inverse * norm_gain).astype(BF16)
        normed_modes = jnp.concatenate([normed * masks[index] for index in range(modes)], axis=1)
        conv_in = product(normed_modes, conv_weight.reshape(modes * width, inner), 1, 0).astype(BF16)
        gate_in = product(normed_modes, gate_weight.reshape(modes * width, inner), 1, 0)
    conv_in = conv_in.reshape(seqs, local_len, inner)
    g_gated = product(g_mix, full_out, 1, 1)

    def terms_of(lefts, grads):
        return jnp.stack([product(left, grads, 1, 0) for left in lefts]).astype(BF16)

    def summed(terms):
        return lax.psum_scatter(terms, "ctx", scatter_dimension=1, tiled=True).astype(jnp.float32)

    edge = from_behind(conv_in[:, local_len - reach :], "ctx", 1)
    extended = jnp.concatenate([edge, conv_in], axis=1).astype(jnp.float32)
    offset = lax.axis_index("ctx") * local_len
    padded = jnp.concatenate([jnp.full((seqs, reach), -1, jnp.int32), segments], axis=1)
    seg_ext = lax.dynamic_slice_in_dim(padded, offset, local_len + reach, 1)
    own_seg = seg_ext[:, reach:]
    same = [
        (seg_ext[:, reach - lag : reach - lag + local_len] == own_seg).astype(jnp.float32)[:, :, None]
        for lag in range(reach + 1)
    ]
    taps = [extended[:, reach - lag : reach - lag + local_len] for lag in range(reach + 1)]
    pre = jnp.zeros((seqs, local_len, inner), jnp.float32) + filter_bias
    for lag in range(reach + 1):
        pre = pre + filter_weight[reach - lag] * taps[lag] * same[lag]
    cut = (1.0 - same[1][:, :, 0]) * 1e30
    conv_out = jax.nn.silu(pre).astype(BF16).reshape(rows, inner)
    selected = pair_total(apply_modes(conv_out, full_select, 1))
    delta_low = selected[:, :rank].astype(BF16)
    b_in = selected[:, rank : rank + states]
    c_out = selected[:, rank + states :]
    bias_rows = sum(masks_float[index] * delta_bias[index] for index in range(modes))
    raw = apply_modes(delta_low, full_delta, 0) + bias_rows

    neg_decay = -jnp.exp(decay_log)
    _, blocks, groups = sizes(raw, seqs, states)
    a2 = state_form(neg_decay * LOG2E, blocks, groups)
    if fast:
        flags = jnp.pad(masks[:, :, 0], ((0, 16 - modes), (0, 0)))
        carried, adjoint, (normed_group, g_mix_group, flags) = scan_entering(
            raw, conv_out, gate_in, g_gated, a2, b_in, c_out, cut, normed, g_mix, flags, seqs
        )
        entering = list(zip(carried, adjoint))
        normed_turned = normed_group.T
        x = jnp.stack([normed_turned * flags[index : index + 1] for index in range(modes)] + [g_mix_group.T])
    else:
        entering = [
            exchange_ends(*scan_ends(raw, conv_out, gate_in, g_gated, a2[j], b_in, c_out, cut, seqs, j), "ctx")
            for j in range(blocks)
        ]
        x = group_rows(normed, g_mix, masks[:, :, 0])
    results = [
        scan_both(raw, conv_out, gate_in, g_gated, skip_gain, a2[j], *entering[j], b_in, c_out, cut, seqs, j)
        for j in range(blocks)
    ]
    early = []
    for part in results[: 1 if fast else blocks]:
        gate_all = lax.all_gather(part[1], "shard", axis=0, tiled=True)
        gated_all = lax.all_gather(part[0], "shard", axis=0, tiled=True)
        early.append((terms_of(x[:modes], gate_all), terms_of(x[modes:], gated_all)))
    if fast:
        first = [results[1][1]] + [
            lax.ppermute(results[1][1], "shard", [(i, i ^ k) for i in range(4)]) for k in range(1, 4)
        ]
    early, results = lax.optimization_barrier((early, results))
    gate_grads = [summed(part[0]) for part in early]
    out_grads = [summed(part[1])[0] for part in early]
    gated, g_gate, g_raw, g_conv, g_neg, g_b, g_c, g_skip = zip(*results)
    gated, g_gate, g_raw, g_conv = (jnp.concatenate(part, axis=1) for part in (gated, g_gate, g_raw, g_conv))
    g_skip = jnp.concatenate(g_skip, axis=2)
    g_neg = jnp.stack([jnp.sum(part, axis=0) for part in g_neg])

    mix_part = product(gated, full_out, 1, 0)
    mix_local = half_total(mix_part.astype(BF16), mix_part) * valid_rows
    local_stream = stream.reshape(rows, part_width).astype(jnp.float32)
    output = (local_stream + mix_local).astype(BF16).reshape(seqs, local_len, part_width)
    stream_sq = jnp.sum(valid_rows * jnp.sum(whole * whole, axis=1, keepdims=True))
    count = jnp.sum(valid_rows)
    skip_grad = jnp.sum(g_skip, axis=(0, 1))
    decay_grad = from_state_form(g_neg) * neg_decay
    bias_grad = product(masks[:, :, 0], g_raw, 1, 0)
    delta_terms = modal_terms(delta_low, g_raw)
    g_low = apply_modes(g_raw, full_delta, 1)
    select_part = jnp.concatenate([g_low, pair_sum(sum(g_b), states), pair_sum(sum(g_c), states)], axis=1)
    g_sel_low = pair_total(select_part).astype(BF16)
    select_terms = modal_terms(g_sel_low, conv_out)
    g_conv = g_conv + apply_modes(g_sel_low, full_select, 0)
    sig_pre = jax.nn.sigmoid(pre)
    g_pre = g_conv.reshape(seqs, local_len, inner) * sig_pre * (1.0 + pre * (1.0 - sig_pre))
    offset_grad = jnp.sum(g_pre, axis=(0, 1))
    filter_rows = [None] * (reach + 1)
    g_ext = jnp.zeros((seqs, local_len + reach, inner), jnp.float32)
    for lag in range(reach + 1):
        masked = g_pre * same[lag]
        filter_rows[reach - lag] = jnp.sum(masked * taps[lag], axis=(0, 1))
        g_ext = g_ext + jnp.pad(filter_weight[reach - lag] * masked, ((0, 0), (reach - lag, lag), (0, 0)))
    filter_grad = jnp.stack(filter_rows)
    returned = from_behind(g_ext[:, :reach], "ctx", -1)
    g_conv_in = g_ext[:, reach:] + jnp.pad(returned, ((0, 0), (local_len - reach, 0), (0, 0)))
    g_conv_in = g_conv_in.reshape(rows, inner).astype(BF16)
    if fast:
        final, g_normed_part, other = finish_weights(
            x, first, g_conv_in, results[1][0], results[0][1], masks_float[:, :, 0].T, conv_weight, gate_weight
        )
        halves = [jnp.concatenate([final[i], final[i + 1]], axis=1) for i in range(0, 14, 2)]
        gate_grads.append(jnp.stack(halves[:2]))
        conv_grad = jnp.stack([jnp.concatenate([halves[2 + m], halves[4 + m]], axis=1) for m in range(2)])
        out_grads.append(halves[6])
    else:
        conv_grad = summed(terms_of(x[:modes], lax.all_gather(g_conv_in, "shard", axis=0, tiled=True)))
        g_normed_part = sum(
            product(grad * masks[index], weight[index], 1, 1)
            for weight, grad in ((conv_weight, g_conv_in), (gate_weight, g_gate))
            for index in range(modes)
        )
    in_grad = jnp.stack([conv_grad, jnp.concatenate(gate_grads, axis=2)], axis=2)
    out_grad = jnp.concatenate(out_grads, axis=1).T
    group = lax.axis_size("shard") * lax.axis_size("ctx")
    terms = jnp.concatenate(
        [delta_terms.reshape(modes * group, -1, inner), select_terms.reshape(modes * group, -1, inner)], axis=1
    ).astype(BF16)
    terms = terms.reshape(modes, group, -1, inner).transpose(1, 0, 2, 3).reshape(group, -1, inner)
    terms = jnp.pad(terms, ((0, 0), (0, -terms.shape[1] % 16), (0, 0)))
    terms = lax.psum_scatter(terms, ("shard", "ctx"), scatter_dimension=0, tiled=True)[0].astype(jnp.float32)
    deep = rank // group
    terms = terms[: modes * (terms.shape[0] // modes)]
    each = deep + full_select.shape[1] // group
    terms = terms[: modes * each].reshape(modes, each, inner)
    delta_grad, select_grad = terms[:, :deep], terms[:, deep:]

    row_total = pair_total(jnp.sum(g_normed_part * norm_gain * whole, axis=1, keepdims=True))
    gain_part = jnp.sum(g_normed_part * whole * inverse, axis=0)
    scalars = jnp.stack([stream_sq * (1.0 / tps), jnp.sum(mix_local * mix_local), count * (1.0 / tps)])
    small = jnp.concatenate([bias_grad, decay_grad, skip_grad[None], filter_grad, offset_grad[None]], axis=0)
    if fast and width == inner and small.shape[0] == 24:
        wide = jnp.stack([gain_part, jnp.pad(scalars, (0, width - 3))])
        sums = small_sum(jnp.concatenate([small, jnp.pad(wide, ((0, 6), (0, 0)))], axis=0))
        small_total, gain_total, scalars = sums[:24], sums[24], sums[25, :3]
    else:
        small_total = lax.psum(small, ("shard", "ctx"))
        wide = lax.psum(jnp.concatenate([gain_part, scalars]), ("shard", "ctx", "tp"))
        gain_total, scalars = wide[:width], wide[width:]
    start = lax.axis_index("tp") * part_width
    if fast:
        g_normed = lax.dynamic_slice_in_dim(g_normed_part, start, part_width, 1) + other.astype(jnp.float32)
    else:
        g_normed = lax.psum_scatter(
            g_normed_part.astype(BF16), "tp", scatter_dimension=1, tiled=True
        ).astype(jnp.float32)
    own_gain = lax.dynamic_slice_in_dim(norm_gain, start, part_width, 0)
    g_stream = inverse * own_gain * g_normed - local_stream * inverse**3 * row_total / width
    gain_grad = lax.dynamic_slice_in_dim(gain_total, start, part_width, 0)
    upstream_local = upstream.reshape(rows, part_width).astype(jnp.float32)
    stream_gradient = (upstream_local + g_stream).astype(BF16).reshape(seqs, local_len, part_width)

    denominator = jnp.maximum(scalars[2], 1.0) * width
    stream_rms = jnp.sqrt(scalars[0] / denominator)
    mixer_rms = jnp.sqrt(scalars[1] / denominator)
    return (
        output,
        stream_gradient,
        gain_grad,
        in_grad,
        select_grad,
        delta_grad,
        small_total[:modes],
        out_grad,
        small_total[modes + states + 1 : modes + states + 2 + reach],
        small_total[modes + states + 2 + reach],
        small_total[modes : modes + states],
        small_total[modes + states],
        stream_rms,
        mixer_rms,
    )


def solution(mesh):
    return jax.shard_map(
        per_device,
        mesh=mesh,
        in_specs=(
            P("shard", "ctx", "tp"),
            P(),
            P(None, "shard", None, "tp"),
            P(None, "shard", "tp"),
            P(None, "shard", "tp"),
            P(None, "tp"),
            P("tp", "shard"),
            P(None, "tp"),
            P("tp"),
            P(None, "tp"),
            P("tp"),
            P("shard", None),
            P("shard", "ctx"),
            P("shard", "ctx"),
            P("shard", "ctx", "tp"),
        ),
        out_specs=(
            P("shard", "ctx", "tp"),
            P("shard", "ctx", "tp"),
            P("tp"),
            P(None, ("shard", "ctx"), None, "tp"),
            P(None, ("shard", "ctx"), "tp"),
            P(None, ("shard", "ctx"), "tp"),
            P(None, "tp"),
            P("tp", ("shard", "ctx")),
            P(None, "tp"),
            P("tp"),
            P(None, "tp"),
            P("tp"),
            P(),
            P(),
        ),
        check_vma=False,
    )
```
